128 devices in a mesh: member: 8 (over y, z_lo), token: 16 (over z_hi, x, core).
Axes of the slice: x: 4, y: 4, z: 4 (z_hi: 2, z_lo: 2; z = z_hi * 2 + z_lo), core: 2. Of those that a mesh axis runs over, the one named last changes fastest.
Arguments:
- latents: bfloat16 [2048, 1024], P('token', 'member'), may hold values from -6 to 6
- noise: bfloat16 [32, 2048, 128], P('member', 'token'), may hold values from -6 to 6
- noise_weight: bfloat16 [128, 1024], replicated, may hold values from -0.5 to 0.5
- gain: bfloat16 [1024], replicated, may hold values from 0.25 to 1.75
- w_in: bfloat16 [1024, 4096], replicated, may hold values from -0.1875 to 0.1875
- w_out: bfloat16 [4096, 768], replicated, may hold values from -0.09375 to 0.09375
- observed: bfloat16 [2048, 768], P(('token', 'member')), may hold values from -6 to 6
Outputs:
- grad_w_out: float32 [4096, 768], P(('member', 'token'))
- grad_latents: float32 [2048, 1024], P('token', 'member')
The draws below stay inside these ranges and needn't reach their ends.
All inputs are finite; a program needn't handle non-finite values.
Results may differ from the reference program's by a relative error of at most 0.0012.
Values may be sent and summed in bfloat16 or wider, within the bound.
No kernel may reach another device: no remote copies, remote signals or barrier semaphores. Data moves between devices by JAX's collectives and lax.ppermute only.
A program may use at most 128 MiB of HBM per device.

```python
import jax
import jax.numpy as jnp
from jax import lax

D = 1024
FF = 4096
F = 768
E = 128
MEMBERS = 32
TOKENS = 2048


def shard_levels(rng, shape, pieces, least, top_value):
    def one(dim, shards_of):
        draws = jax.random.uniform(jax.random.fold_in(jax.random.fold_in(rng, 6), dim), (shards_of,), jnp.float32, least / len(pieces), top_value / len(pieces))
        return jnp.repeat(jnp.exp(draws), shape[dim] // shards_of).reshape((-1,) + (1,) * (len(shape) - dim - 1))

    loudness = one(*pieces[0])
    for cut in pieces[1:]:
        loudness = loudness * one(*cut)
    return loudness


def bell_draw(own_key, extent, width, most, pieces=(), held_as=jnp.bfloat16):
    drawn = width * jax.random.normal(own_key, extent, jnp.float32)
    if pieces:
        drawn = drawn * shard_levels(own_key, extent, pieces, -0.22, 0.18)
    return jnp.clip(drawn, -most, most).astype(held_as)


def setup_inputs(seed: int = 0) -> dict:
    splits = jax.random.split(jax.random.key(seed), 8)
    latents = bell_draw(splits[0], (TOKENS, D), 1.0, 6.0, ((0, 16), (1, 8)))
    noise = bell_draw(splits[1], (MEMBERS, TOKENS, E), 1.0, 6.0, ((0, 8), (1, 16)))
    noise_weight = bell_draw(splits[2], (E, D), E ** -0.5, 0.5)
    gain = jnp.clip(1.0 + 0.15 * jax.random.normal(splits[3], (D,), jnp.float32), 0.25, 1.75).astype(jnp.bfloat16)
    w_in = bell_draw(splits[4], (D, FF), D ** -0.5, 0.1875)
    w_out = bell_draw(splits[5], (FF, F), FF ** -0.5, 0.09375)
    observed = bell_draw(splits[6], (TOKENS, F), 1.0, 6.0, ((0, 128),))
    return dict(latents=latents, noise=noise, noise_weight=noise_weight, gain=gain, w_in=w_in, w_out=w_out, observed=observed)


def gelu_tanh(values):
    return jax.nn.gelu(values, approximate=True)

def forward_member(latents, noise_one, noise_weight, gain, w_in):
    cond = latents.astype(jnp.float32) + jnp.dot(noise_one, noise_weight, preferred_element_type=jnp.float32)
    scale = lax.rsqrt(lax.optimization_barrier(jnp.mean(cond * cond, axis=-1, keepdims=True)) + 1e-05)
    normed = (cond * scale * gain.astype(jnp.float32)).astype(jnp.bfloat16)
    pre = jnp.dot(normed, w_in, preferred_element_type=jnp.float32)
    hidden = gelu_tanh(pre).astype(jnp.bfloat16)
    return (cond, scale, pre, hidden)

def score_one(own, every, target):
    err = own - target
    enorm = jnp.sqrt(lax.optimization_barrier(jnp.mean(err * err, axis=-1, keepdims=True)) + 1e-06)
    diff = own[None] - every
    dist = jnp.sqrt(lax.optimization_barrier(jnp.mean(diff * diff, axis=-1, keepdims=True)) + 1e-06)
    spread = lax.optimization_barrier(jnp.sum(diff / dist, axis=0)) / every.shape[0]
    return err / enorm - spread

def reference(latents, noise, noise_weight, gain, w_in, w_out, observed):

    def predict(noise_one):
        cond, scale, pre, hidden = forward_member(latents, noise_one, noise_weight, gain, w_in)
        return jnp.dot(hidden, w_out, preferred_element_type=jnp.float32).astype(jnp.bfloat16)
    pred = lax.map(predict, noise)
    every = pred.astype(jnp.float32)
    target = observed.astype(jnp.float32)
    score_grad = lax.map(lambda own: score_one(own, every, target), every)
    w_out_f = w_out.astype(jnp.float32)

    def backward(carry, inputs):
        grad_out, grad_lat = carry
        noise_one, grad_one = inputs
        cond, scale, pre, hidden = forward_member(latents, noise_one, noise_weight, gain, w_in)
        grad_out = grad_out + jnp.dot(hidden.astype(jnp.float32).T, grad_one, preferred_element_type=jnp.float32, precision=lax.Precision.HIGHEST)
        dhidden = jnp.dot(grad_one, w_out_f.T, preferred_element_type=jnp.float32, precision=lax.Precision.HIGHEST)
        _, pullback = jax.vjp(gelu_tanh, pre)
        dpre = pullback(dhidden)[0].astype(jnp.bfloat16)
        dnormed = jnp.dot(dpre, w_in.T, preferred_element_type=jnp.float32)
        weighted = dnormed * gain.astype(jnp.float32)
        dcond = scale * weighted - cond * scale ** 3 * lax.optimization_barrier(jnp.mean(weighted * cond, axis=-1, keepdims=True))
        return ((grad_out, grad_lat + dcond), None)
    start = (jnp.zeros((FF, F), jnp.float32), jnp.zeros((TOKENS, D), jnp.float32))
    (grad_w_out, grad_latents), _ = lax.scan(backward, start, (noise, score_grad))
    return (grad_w_out, grad_latents)
```

```python
import functools

import jax
import jax.numpy as jnp
import numpy as np
from jax import lax
from jax.experimental import pallas as pl
from jax.experimental.pallas import tpu as pltpu
from jax.sharding import PartitionSpec as P

AXES = ("member", "token")
FIRST = (("x0", "y0", "z0"), ("x1", "y1", "z1"))
VMEM = 56 * 1024 * 1024


def coords(index):
    member, token = divmod(index, 16)
    y, z_lo = divmod(member, 2)
    z_hi, x, core = token // 8, token // 2 % 4, token % 2
    return {"x": x, "y": y, "z": 2 * z_hi + z_lo}, core


def index_of(place, core):
    return (place["y"] * 2 + place["z"] % 2) * 16 + (place["z"] // 2) * 8 + place["x"] * 2 + core


def chip_bits(chip):
    place, _ = coords(2 * chip)
    bits = {}
    for axis in "xyz":
        value = place[axis]
        bits[axis + "0"] = (value & 1) ^ (value >> 1)
        bits[axis + "1"] = value >> 1
    return bits


def order_of(core, part):
    first = FIRST[core]
    return first[part:] + first[:part] + FIRST[1 - core]


def positions():
    table = np.zeros((128, 3, 64), np.int32)
    bits = [chip_bits(chip) for chip in range(64)]
    for device in range(128):
        mine = bits[device // 2]
        for part in range(3):
            order = order_of(device % 2, part)
            for chip in range(64):
                place = 0
                for dim in order:
                    place = 2 * place + (mine[dim] ^ bits[chip][dim])
                table[device, part, chip] = place
    return table.reshape(128, 192)


def partner(index, dim):
    place, core = coords(index)
    place[dim[0]] ^= 1 if dim[1] == "0" else 3
    return index_of(place, core)


def swap_stage(values, part, stage):
    pairs = [(i, partner(i, order_of(i % 2, part)[stage])) for i in range(128)]
    return lax.ppermute(values, AXES, pairs)


def swap_core(values):
    return lax.ppermute(values, AXES, [(i, i ^ 1) for i in range(128)])


def params(**more):
    return pltpu.CompilerParams(vmem_limit_bytes=VMEM, **more)


def hidden_kernel(moved_ref, nw_ref, gain_ref, w_in_ref, cond_ref, scale_ref, hidden_ref, slope_ref, normed_ref):
    @pl.when(pl.program_id(0) == 0)
    def _():
        moved = moved_ref[...]
        noise = moved[:, :4].reshape(512, 128)
        latents = jnp.concatenate([moved[j, 4] for j in range(8)], axis=1).astype(jnp.float32)
        cond = jnp.dot(noise, nw_ref[...], preferred_element_type=jnp.float32)
        cond = (cond.reshape(32, 16, 1024) + latents[None]).reshape(512, 1024)
        scale = lax.rsqrt(jnp.mean(cond * cond, axis=-1, keepdims=True) + 1e-05)
        cond_ref[...] = cond
        scale_ref[...] = scale
        normed_ref[...] = (cond * scale * gain_ref[...].astype(jnp.float32)).astype(jnp.bfloat16)

    pre = jnp.dot(normed_ref[...], w_in_ref[...], preferred_element_type=jnp.float32)
    root = np.float32(np.sqrt(2 / np.pi))
    cubic = np.float32(np.sqrt(2 / np.pi) * 0.044715)
    square = pre * pre
    half = 0.5 * pre
    bend = jnp.tanh(pre * (root + cubic * square))
    hidden_ref[...] = (half + half * bend).astype(jnp.bfloat16)
    slope_ref[...] = 0.5 + 0.5 * bend + half * (1.0 - bend * bend) * (root + 3.0 * cubic * square)


def make_hidden(moved, noise_weight, gain, w_in, chunk=512):
    steps = 4096 // chunk
    whole = lambda *shape: pl.BlockSpec(shape, lambda i: (0,) * len(shape))
    return pl.pallas_call(
        hidden_kernel,
        grid=(steps,),
        in_specs=[
            whole(8, 5, 16, 128),
            whole(128, 1024),
            whole(1, 1024),
            pl.BlockSpec((1024, chunk), lambda i: (0, i)),
        ],
        out_specs=[
            whole(512, 1024),
            whole(512, 1),
            pl.BlockSpec((512, chunk), lambda i: (0, i)),
            pl.BlockSpec((512, chunk), lambda i: (0, i)),
        ],
        out_shape=[
            jax.ShapeDtypeStruct((512, 1024), jnp.float32),
            jax.ShapeDtypeStruct((512, 1), jnp.float32),
            jax.ShapeDtypeStruct((512, 4096), jnp.bfloat16),
            jax.ShapeDtypeStruct((512, 4096), jnp.float32),
        ],
        scratch_shapes=[pltpu.VMEM((512, 1024), jnp.bfloat16)],
        compiler_params=params(),
        cost_estimate=pl.CostEstimate(flops=2 * 512 * 1024 * 4096, bytes_accessed=24 << 20, transcendentals=1 << 21),
        name="hidden_rows",
    )(moved, noise_weight, gain, w_in)


def score_kernel(core_ref, hidden_ref, w_out_ref, target_ref, high_ref, low_ref, own_ref, other_ref, total_ref, pred_ref, grad_ref):
    step = pl.program_id(0)
    term = jnp.dot(hidden_ref[...], w_out_ref[...], preferred_element_type=jnp.float32)

    @pl.when(step == 0)
    def _():
        total_ref[...] = term

    @pl.when(step > 0)
    def _():
        total_ref[...] += term

    @pl.when(step == pl.num_programs(0) - 1)
    def _():
        pred_ref[...] = total_ref[...].astype(jnp.bfloat16).astype(jnp.float32).reshape(32, 16, 768)
        grad_ref[...] = jnp.zeros_like(grad_ref)

        def pair(member, own, other, total):
            diff = own - pred_ref[other]
            inverse = lax.rsqrt(jnp.mean(diff * diff, axis=-1, keepdims=True) + 1e-06)
            push = diff * inverse
            grad_ref[other] -= push
            return total + push

        def ring(member, carry):
            own = pred_ref[member]
            total = jnp.zeros((16, 768), jnp.float32)
            for offset in range(1, 16):
                total = pair(member, own, lax.rem(member + offset, 32), total)
            grad_ref[member] += total
            return carry

        def opposite(member, carry):
            grad_ref[member] += pair(member, pred_ref[member], member + 16, jnp.zeros((16, 768), jnp.float32))
            return carry

        lax.fori_loop(0, 32, ring, 0)
        lax.fori_loop(0, 16, opposite, 0)
        err = pred_ref[...] - target_ref[...].astype(jnp.float32)[None]
        inverse = lax.rsqrt(jnp.mean(err * err, axis=-1, keepdims=True) + 1e-06)
        grad = (err * inverse - grad_ref[...] * (1.0 / 32)).reshape(512, 768)
        high = grad.astype(jnp.bfloat16)
        low = (grad - high.astype(jnp.float32)).astype(jnp.bfloat16)
        high_ref[...] = high
        low_ref[...] = low

        def halves(mine_ref, yours_ref):
            mine_ref[:, :384] = high[:, :384]
            mine_ref[:, 384:] = low[:, :384]
            yours_ref[:, :384] = high[:, 384:]
            yours_ref[:, 384:] = low[:, 384:]

        @pl.when(core_ref[0] == 0)
        def _():
            halves(own_ref, other_ref)

        @pl.when(core_ref[0] == 1)
        def _():
            halves(other_ref, own_ref)


def make_score(core, hidden, w_out, observed, chunk=512):
    whole = lambda *shape: pl.BlockSpec(shape, lambda i, c: (0,) * len(shape))
    return pl.pallas_call(
        score_kernel,
        grid_spec=pltpu.PrefetchScalarGridSpec(
            num_scalar_prefetch=1,
            grid=(4096 // chunk,),
            in_specs=[
                pl.BlockSpec((512, chunk), lambda i, c: (0, i)),
                pl.BlockSpec((chunk, 768), lambda i, c: (i, 0)),
                whole(16, 768),
            ],
            out_specs=[whole(512, 768)] * 4,
            scratch_shapes=[
                pltpu.VMEM((512, 768), jnp.float32),
                pltpu.VMEM((32, 16, 768), jnp.float32),
                pltpu.VMEM((32, 16, 768), jnp.float32),
            ],
        ),
        out_shape=[jax.ShapeDtypeStruct((512, 768), jnp.bfloat16)] * 4,
        compiler_params=params(),
        cost_estimate=pl.CostEstimate(flops=2 * 512 * 768 * 4096 * 3, bytes_accessed=14 << 20, transcendentals=0),
        name="score_rows",
    )(core, hidden, w_out, observed)


def outer_kernel(places_ref, mine_ref, theirs_ref, own_ref, got_ref, *outs):
    sums = (((0,), (0,)), ((), ()))
    both = lax.dot_general(mine_ref[...], own_ref[...], sums, preferred_element_type=jnp.float32)
    both += lax.dot_general(theirs_ref[...], got_ref[...], sums, preferred_element_type=jnp.float32)
    result = both[:, :384] + both[:, 384:]
    blocks = result.shape[0] // 64
    for block in range(blocks):
        for part in range(3):
            place = places_ref[part * 64 + pl.program_id(0) * blocks + block]
            piece = result[block * 64 : block * 64 + 64, part * 128 : part * 128 + 128]

            @pl.when(place < 32)
            def _():
                outs[part][pl.ds(pl.multiple_of(place * 64, 64), 64), :] = piece

            @pl.when(place >= 32)
            def _():
                outs[3 + part][pl.ds(pl.multiple_of((place - 32) * 64, 64), 64), :] = piece


def make_outer(places, mine, theirs, own, got, chunk=256):
    whole = lambda *shape: pl.BlockSpec(shape, lambda i, c: (0,) * len(shape))
    return pl.pallas_call(
        outer_kernel,
        grid_spec=pltpu.PrefetchScalarGridSpec(
            num_scalar_prefetch=1,
            grid=(4096 // chunk,),
            in_specs=[
                pl.BlockSpec((512, chunk), lambda i, c: (0, i)),
                pl.BlockSpec((512, chunk), lambda i, c: (0, i)),
                whole(512, 768),
                whole(512, 768),
            ],
            out_specs=[whole(2048, 128)] * 6,
        ),
        out_shape=[jax.ShapeDtypeStruct((2048, 128), jnp.float32)] * 6,
        compiler_params=params(),
        cost_estimate=pl.CostEstimate(flops=2 * 1024 * 768 * 4096, bytes_accessed=16 << 20, transcendentals=0),
        name="outer_rows",
    )(places, mine, theirs, own, got)


def back_kernel(high_ref, low_ref, w_out_ref, w_in_ref, slope_ref, cond_ref, scale_ref, gain_ref, out_ref, total_ref):
    step = pl.program_id(0)
    last = (((1,), (1,)), ((), ()))
    w_out = w_out_ref[...]
    back = lax.dot_general(high_ref[...], w_out, last, preferred_element_type=jnp.float32)
    back += lax.dot_general(low_ref[...], w_out, last, preferred_element_type=jnp.float32)
    dpre = (back * slope_ref[...]).astype(jnp.bfloat16)
    term = lax.dot_general(dpre, w_in_ref[...], last, preferred_element_type=jnp.float32)

    @pl.when(step == 0)
    def _():
        total_ref[...] = term

    @pl.when(step > 0)
    def _():
        total_ref[...] += term

    @pl.when(step == pl.num_programs(0) - 1)
    def _():
        cond = cond_ref[...]
        scale = scale_ref[...]
        weighted = total_ref[...] * gain_ref[...].astype(jnp.float32)
        mean = jnp.mean(weighted * cond, axis=-1, keepdims=True)
        dcond = scale * weighted - cond * (scale * scale * scale * mean)
        out_ref[...] = jnp.sum(dcond.reshape(32, 16, 1024), axis=0)


def make_back(high, low, w_out, w_in, slope, cond, scale, gain, chunk=512):
    whole = lambda *shape: pl.BlockSpec(shape, lambda i: (0,) * len(shape))
    return pl.pallas_call(
        back_kernel,
        grid=(4096 // chunk,),
        in_specs=[
            whole(512, 768),
            whole(512, 768),
            pl.BlockSpec((chunk, 768), lambda i: (i, 0)),
            pl.BlockSpec((1024, chunk), lambda i: (0, i)),
            pl.BlockSpec((512, chunk), lambda i: (0, i)),
            whole(512, 1024),
            whole(512, 1),
            whole(1, 1024),
        ],
        out_specs=whole(16, 1024),
        out_shape=jax.ShapeDtypeStruct((16, 1024), jnp.float32),
        scratch_shapes=[pltpu.VMEM((512, 1024), jnp.float32)],
        compiler_params=params(),
        cost_estimate=pl.CostEstimate(flops=2 * 512 * 4096 * (768 * 2 + 1024), bytes_accessed=28 << 20, transcendentals=0),
        name="back_rows",
    )(high, low, w_out, w_in, slope, cond, scale, gain)


def per_device(latents, noise, noise_weight, gain, w_in, w_out, observed):
    device = lax.axis_index(AXES)
    places = lax.dynamic_index_in_dim(jnp.asarray(positions()), device, 0, keepdims=False)
    core = (device % 2).reshape(1)
    gain = gain.reshape(1, 1024)

    moved = jnp.concatenate([noise, latents[None]], axis=0)
    moved = lax.all_to_all(moved, "member", split_axis=1, concat_axis=0, tiled=True)
    cond, scale, hidden, slope = make_hidden(moved.reshape(8, 5, 16, 128), noise_weight, gain, w_in)
    theirs = swap_core(hidden)
    high, low, own, other = make_score(core, hidden, w_out, observed)
    got = swap_core(other)
    outs = make_outer(places, hidden, theirs, own, got)
    keep, send = list(outs[:3]), list(outs[3:])

    latent_sum = make_back(high, low, w_out, w_in, slope, cond, scale, gain)
    grad_latents = lax.all_to_all(latent_sum, "member", split_axis=1, concat_axis=0, tiled=True)

    for stage in range(2):
        came = [swap_stage(send[part], part, stage) for part in range(3)]
        rows = 1024 >> stage
        send = [keep[part][rows:] + came[part][rows:] for part in range(3)]
        keep = [keep[part][:rows] + came[part][:rows] for part in range(3)]
    came = [swap_stage(send[part], part, 2) for part in range(3)]
    rows = 256
    send = jnp.concatenate([keep[part][rows:] + came[part][rows:] for part in range(3)], axis=1)
    keep = jnp.concatenate([keep[part][:rows] + came[part][:rows] for part in range(3)], axis=1)
    for stage in range(3, 6):
        came = swap_stage(send, 0, stage)
        rows = rows // 2
        if stage < 5:
            send, keep = keep[rows:] + came[rows:], keep[:rows] + came[:rows]
    block = keep + came
    top, bottom = block[:32], block[32:]
    first = core[0] == 0
    mine = jnp.where(first, top, bottom)
    given = swap_core(jnp.where(first, bottom, top))
    grad_w_out = jnp.where(
        first, jnp.concatenate([mine, given], axis=1), jnp.concatenate([given, mine], axis=1)
    )
    return (grad_w_out, grad_latents)


def solution(mesh):
    placed = (
        P("token", "member"),
        P("member", "token", None),
        P(),
        P(),
        P(),
        P(),
        P(("token", "member"), None),
    )
    return jax.shard_map(
        per_device,
        mesh=mesh,
        in_specs=placed,
        out_specs=(P(("member", "token"), None), P("token", "member")),
        check_vma=False,
    )
```

```python
import functools

import jax
import jax.numpy as jnp
import numpy as np
from jax import lax
from jax.experimental import pallas as pl
from jax.experimental.pallas import tpu as pltpu
from jax.sharding import PartitionSpec as P

AXES = ("member", "token")
FIRST = (("x0", "x1", "z1"), ("y0", "y1", "z0"))
CHUNK = 512
STEPS = 4096 // CHUNK
F32, BF16 = jnp.float32, jnp.bfloat16
LAST = (((1,), (1,)), ((), ()))


def coords(index):
    member, token = divmod(index, 16)
    y, z_lo = divmod(member, 2)
    z_hi, x, core = token // 8, token // 2 % 4, token % 2
    return {"x": x, "y": y, "z": 2 * z_hi + z_lo}, core


def index_of(place, core):
    return (place["y"] * 2 + place["z"] % 2) * 16 + (place["z"] // 2) * 8 + place["x"] * 2 + core


def chip_bits(chip):
    place, _ = coords(2 * chip)
    bits = {}
    for axis in "xyz":
        value = place[axis]
        bits[axis + "0"] = (value & 1) ^ (value >> 1)
        bits[axis + "1"] = value >> 1
    return bits


def order_of(core, part):
    return FIRST[core][part:] + FIRST[core][:part]


def group_place(index):
    place, core = coords(index)
    if core == 0:
        return (0, place["x"], place["z"] // 2), place["y"] * 2 + place["z"] % 2
    return (1, place["y"], place["z"] % 2 ^ place["z"] // 2), place["z"] // 2 * 4 + place["x"]


def last_groups():
    groups = {}
    for index in range(128):
        group, at = group_place(index)
        groups.setdefault(group, [None] * 8)[at] = index
    return [groups[name] for name in sorted(groups)]


def chip_table():
    table = np.zeros((128, 3, 64), np.int32)
    bits = [chip_bits(chip) for chip in range(64)]
    for device in range(128):
        mine, core = bits[device // 2], device % 2
        for part in range(3):
            for chip in range(64):
                place = 0
                for dim in order_of(core, part):
                    place = 2 * place + (mine[dim] ^ bits[chip][dim])
                table[device, part, 8 * place + group_place(2 * chip + core)[1]] = chip
    return table.reshape(128, 192)


def partner(index, dim):
    place, core = coords(index)
    place[dim[0]] ^= 1 if dim[1] == "0" else 3
    return index_of(place, core)


def swap_stage(values, part, stage):
    pairs = [(i, partner(i, order_of(i % 2, part)[stage])) for i in range(128)]
    return lax.ppermute(values, AXES, pairs)


def swap_core(values):
    return lax.ppermute(values, AXES, [(i, i ^ 1) for i in range(128)])


def call(body, name, outs, args, spaces, out_spaces, scratch=(), flops=0, limit=16):
    placed = [
        pltpu.with_memory_space_constraint(a, {"v": pltpu.VMEM, "a": pltpu.HBM}[space]) if space in "va" else a
        for a, space in zip(args, spaces)
    ]
    kinds = {"s": pltpu.SMEM, "v": pltpu.VMEM, "m": pltpu.VMEM, "a": pltpu.HBM, "h": pltpu.HBM}
    return pl.pallas_call(
        body,
        in_specs=[pl.BlockSpec(memory_space=kinds[space]) for space in spaces],
        out_specs=[pl.BlockSpec(memory_space=kinds[space]) for space in out_spaces],
        out_shape=[
            {"v": pltpu.VMEM, "h": pltpu.HBM, "m": jax.ShapeDtypeStruct}[space](shape, kind)
            for (shape, kind), space in zip(outs, out_spaces)
        ],
        scratch_shapes=list(scratch),
        compiler_params=pltpu.CompilerParams(vmem_limit_bytes=limit * 1024 * 1024),
        cost_estimate=pl.CostEstimate(
            flops=flops, bytes_accessed=sum(a.size * a.dtype.itemsize for a in args), transcendentals=0
        ),
        name=name,
    )(*placed)


def gather_kernel(noise_ref, latents_ref, out_ref):
    for j in range(8):
        rows = slice(j * 16, j * 16 + 16)
        for i in range(4):
            out_ref[j, i] = noise_ref[i, rows, :]
        out_ref[j, 4] = latents_ref[rows, :]


def forward_kernel(moved_ref, nw_hbm, gain_ref, w_in_hbm, w_out_hbm, cond_hbm, slope_hbm, pred_ref, *rest):
    turned = rest[:4]
    cond_ref, slope_ref, pre_ref, total_ref, out_sems, cond_sem = rest[4:10]
    w_in_ref, w_out_ref, nw_ref, in_sems, mid_sems, nw_sem = rest[10:]

    def columns(step):
        return slice(step * CHUNK, (step + 1) * CHUNK)

    def put(step):
        return pltpu.make_async_copy(slope_ref.at[step], slope_hbm.at[step], out_sems.at[step])

    def fetch_in(half):
        return [
            pltpu.make_async_copy(
                w_in_hbm.at[i * 256 : i * 256 + 256, half * 2048 : half * 2048 + 2048],
                w_in_ref.at[i * 256 : i * 256 + 256, half * 2048 : half * 2048 + 2048],
                in_sems.at[half, i],
            )
            for i in range(4)
        ]

    def fetch_out(step):
        return pltpu.make_async_copy(w_out_hbm.at[columns(step), :], w_out_ref.at[columns(step), :], mid_sems.at[step])

    fetch_nw = pltpu.make_async_copy(nw_hbm, nw_ref, nw_sem)
    fetch_nw.start()
    for copy in fetch_in(0):
        copy.start()
    for step in range(STEPS // 2):
        fetch_out(step).start()
    for copy in fetch_in(1):
        copy.start()
    for step in range(STEPS // 2, STEPS):
        fetch_out(step).start()
    moved = moved_ref[...]
    noise = moved[:, :4].reshape(512, 128)
    latents = jnp.concatenate([moved[j, 4] for j in range(8)], axis=1).astype(F32)
    fetch_nw.wait()
    cond = jnp.dot(noise, nw_ref[...], preferred_element_type=F32)
    cond = (cond.reshape(32, 16, 1024) + latents[None]).reshape(512, 1024)
    scale = lax.rsqrt(jnp.mean(cond * cond, axis=-1, keepdims=True) + 1e-05)
    cond_ref[...] = cond
    put_cond = pltpu.make_async_copy(cond_ref, cond_hbm, cond_sem)
    put_cond.start()
    normed = (cond * scale * gain_ref[...].astype(F32)).astype(BF16)
    root = np.float32(np.sqrt(2 / np.pi))
    cubic = np.float32(np.sqrt(2 / np.pi) * 0.044715)
    for step in range(STEPS + 1):
        if step in (0, STEPS // 2):
            for copy in fetch_in(step // (STEPS // 2)):
                copy.wait()
        if step < STEPS:
            pre_ref[step % 2] = jnp.dot(normed, w_in_ref[:, columns(step)], preferred_element_type=F32)
        if step > 0:
            done = step - 1
            pre = pre_ref[done % 2]
            square = pre * pre
            bend = jnp.tanh(pre * (root + cubic * square))
            cdf = 0.5 + 0.5 * bend
            value = pre * cdf
            hidden = value.astype(BF16)
            slope_ref[done] = cdf + (value - value * cdf) * (2.0 * root + 6.0 * cubic * square)
            flipped = hidden.T.reshape(8, 4, 16, 512)
            for i in range(4):
                turned[i][done * 128 : done * 128 + 128, :] = flipped[:, i].reshape(128, 512)
            put(done).start()
            fetch_out(done).wait()
            term = jnp.dot(hidden, w_out_ref[columns(done), :], preferred_element_type=F32)
            if done == 0:
                total_ref[...] = term
            elif done < STEPS - 1:
                total_ref[...] += term
            else:
                pred_ref[...] = (total_ref[...] + term).astype(BF16)
    put_cond.wait()
    for step in range(STEPS):
        put(step).wait()


def score_kernel(core_ref, pred_in_ref, target_ref, high_hbm, low_hbm, own_ref, other_ref, pred_ref, grad_ref, high_ref, low_ref, sems):
    pred_ref[...] = pred_in_ref[...].astype(F32).reshape(32, 16, 768)
    grad_ref[...] = jnp.zeros_like(grad_ref)

    def pair(own, other, total):
        diff = own - pred_ref[other]
        inverse = lax.rsqrt(jnp.mean(diff * diff, axis=-1, keepdims=True) + 1e-06)
        push = diff * inverse
        grad_ref[other] -= push
        return total + push

    def ring(member, carry):
        own = pred_ref[member]
        total = jnp.zeros((16, 768), F32)
        for offset in range(1, 16):
            total = pair(own, lax.rem(member + offset, 32), total)
        grad_ref[member] += total
        return carry

    def opposite(step, carry):
        for i in range(4):
            member = step * 4 + i
            grad_ref[member] += pair(pred_ref[member], member + 16, jnp.zeros((16, 768), F32))
        return carry

    lax.fori_loop(0, 32, ring, 0)
    lax.fori_loop(0, 4, opposite, 0)
    err = pred_ref[...] - target_ref[...].astype(F32)[None]
    inverse = lax.rsqrt(jnp.mean(err * err, axis=-1, keepdims=True) + 1e-06)
    grad = (err * inverse - grad_ref[...] * (1.0 / 32)).reshape(512, 768)
    high = grad.astype(BF16)
    low = (grad - high.astype(F32)).astype(BF16)
    high_ref[...] = high
    low_ref[...] = low
    copies = [
        pltpu.make_async_copy(high_ref, high_hbm, sems.at[0]),
        pltpu.make_async_copy(low_ref, low_hbm, sems.at[1]),
    ]
    for copy in copies:
        copy.start()

    def halves(mine_ref, yours_ref):
        for part in range(3):
            at = part * 128
            mine_ref[:, 2 * at : 2 * at + 128] = high[:, at : at + 128]
            mine_ref[:, 2 * at + 128 : 2 * at + 256] = low[:, at : at + 128]
            yours_ref[:, 2 * at : 2 * at + 128] = high[:, 384 + at : 512 + at]
            yours_ref[:, 2 * at + 128 : 2 * at + 256] = low[:, 384 + at : 512 + at]

    @pl.when(core_ref[0] == 0)
    def _():
        halves(own_ref, other_ref)

    @pl.when(core_ref[0] == 1)
    def _():
        halves(other_ref, own_ref)

    for copy in copies:
        copy.wait()


def outer_kernel(parts, side, chips_ref, own_ref, got_ref, *rest):
    mine, theirs, rest = rest[:4], rest[4:8], rest[8:]
    outs, (a_ref, b_ref) = rest[: len(parts)], rest[len(parts) :]
    for slot, part in enumerate(parts):
        fields = slice(part * 256, part * 256 + 256)
        for quarter in range(4):
            at = slice(quarter * 512, quarter * 512 + 512)
            for block in range(8):
                chip = chips_ref[part * 64 + side * 32 + quarter * 8 + block]
                rows = pl.ds(pl.multiple_of(chip * 16, 16), 16)
                for i in range(4):
                    first = quarter * 512 + block * 64 + i * 16
                    a_ref[first : first + 16, :] = mine[i][rows, :]
                    b_ref[first : first + 16, :] = theirs[i][rows, :]
            both = jnp.dot(a_ref[at, :], own_ref[:, fields], preferred_element_type=F32)
            both += jnp.dot(b_ref[at, :], got_ref[:, fields], preferred_element_type=F32)
            outs[slot][at, :] = both[:, :128] + both[:, 128:]


def make_outer(parts, side, chips, mine, theirs, own, got):
    n = len(parts)
    return call(
        functools.partial(outer_kernel, parts, side),
        "outer_send" if side else "outer_keep",
        [((2048, 128), F32)] * n,
        (chips, own, got, *mine, *theirs),
        "smm" + "m" * 8,
        "m" * n,
        [pltpu.VMEM((2048, 512), BF16)] * 2,
        flops=2 * 1024 * 256 * 2048 * n,
        limit=8,
    )


def back_kernel(begin, high_ref, low_ref, w_out_ref, w_in_ref, slope_ref, *rest):
    if begin == 0:
        (total_ref,) = rest
    else:
        before_ref, cond_ref, gain_ref, out_ref, total_ref = rest
    for step in range(begin, begin + STEPS // 2):
        columns = slice(step * CHUNK, (step + 1) * CHUNK)
        w_out = w_out_ref[columns, :]
        back = lax.dot_general(high_ref[...], w_out, LAST, preferred_element_type=F32)
        back += lax.dot_general(low_ref[...], w_out, LAST, preferred_element_type=F32)
        dpre = (back * slope_ref[step]).astype(BF16)
        term = lax.dot_general(dpre, w_in_ref[:, columns], LAST, preferred_element_type=F32)
        if step == 0:
            total_ref[...] = term
        elif step == begin:
            total_ref[...] = before_ref[...] + term
        else:
            total_ref[...] += term
    if begin == 0:
        return
    cond = cond_ref[...]
    scale = lax.rsqrt(jnp.mean(cond * cond, axis=-1, keepdims=True) + 1e-05)
    weighted = total_ref[...] * gain_ref[...].astype(F32)
    mean = jnp.mean(weighted * cond, axis=-1, keepdims=True)
    dcond = scale * weighted - cond * (scale * scale * scale * mean)
    total = jnp.sum(dcond.reshape(32, 16, 1024), axis=0)
    for j in range(8):
        out_ref[j] = total[:, j * 128 : j * 128 + 128]


def make_back(begin, high, low, w_out, w_in, slope, *more):
    (out,) = call(
        functools.partial(back_kernel, begin),
        "back_end" if begin else "back_begin",
        [((8, 16, 128) if begin else (512, 1024), F32)],
        (high, low, w_out, w_in, slope) + more,
        "m" * (5 + len(more)),
        "m",
        [pltpu.VMEM((512, 1024), F32)] if begin else [],
        flops=512 * 4096 * (768 * 2 + 1024),
        limit=10,
    )
    return out


def pack_kernel(*refs):
    keep, came, (mine_ref, theirs_ref, out_ref) = refs[:3], refs[3:6], refs[6:]
    for part in range(3):
        for j in range(8):
            rows = slice(j * 64, j * 64 + 64)
            out_ref[j, part * 64 : part * 64 + 64, :] = keep[part][rows, :] + came[part][rows, :]
    out_ref[:, 192:208, :] = mine_ref[...]
    out_ref[:, 208:224, :] = theirs_ref[...]


def sum_kernel(core_ref, got_ref, mine_ref, give_ref, latent_ref):
    total = got_ref[0, :192, :]
    for j in range(1, 8):
        total += got_ref[j, :192, :]
    latent_ref[...] = got_ref[:, 192:208, :].reshape(128, 128)
    give_ref[96:, :] = got_ref[:, 208:224, :].reshape(128, 128)
    low = core_ref[0] == 0
    for part in range(3):
        top = total[part * 64 : part * 64 + 32]
        bottom = total[part * 64 + 32 : part * 64 + 64]
        mine_ref[part * 32 : part * 32 + 32, :] = jnp.where(low, top, bottom)
        give_ref[part * 32 : part * 32 + 32, :] = jnp.where(low, bottom, top)


def place_kernel(core_ref, mine_ref, given_ref, latent_ref, grad_ref, out_ref):
    low = core_ref[0] == 0
    for part in range(3):
        mine = mine_ref[part * 32 : part * 32 + 32, :]
        given = given_ref[part * 32 : part * 32 + 32, :]
        grad_ref[:, part * 128 : part * 128 + 128] = jnp.where(low, mine, given)
        grad_ref[:, 384 + part * 128 : 512 + part * 128] = jnp.where(low, given, mine)
    out_ref[...] = jnp.where(low, latent_ref[...], given_ref[96:, :])


def per_device(latents, noise, noise_weight, gain, w_in, w_out, observed):
    device = lax.axis_index(AXES)
    chips = lax.dynamic_index_in_dim(jnp.asarray(chip_table()), device, 0, keepdims=False)
    core = (device % 2).reshape(1)
    gain = gain.reshape(1, 1024)

    noise, latents, chips, core = lax.optimization_barrier((noise, latents, chips, core))
    (moved,) = call(gather_kernel, "gather_in", [((8, 5, 16, 128), BF16)], (noise, latents), "mm", "m")
    moved = lax.all_to_all(moved, "member", split_axis=0, concat_axis=0, tiled=True)
    cond, slope, pred, *turned = call(
        forward_kernel,
        "forward_rows",
        [((512, 1024), F32), ((STEPS, 512, CHUNK), F32), ((512, 768), BF16)] + [((1024, 512), BF16)] * 4,
        (moved, noise_weight, gain, w_in, w_out),
        "mamaa",
        "hhmmmmm",
        [
            pltpu.VMEM((512, 1024), F32),
            pltpu.VMEM((STEPS, 512, CHUNK), F32),
            pltpu.VMEM((2, 512, CHUNK), F32),
            pltpu.VMEM((512, 768), F32),
            pltpu.SemaphoreType.DMA((STEPS,)),
            pltpu.SemaphoreType.DMA,
            pltpu.VMEM((1024, 4096), BF16),
            pltpu.VMEM((4096, 768), BF16),
            pltpu.VMEM((128, 1024), BF16),
            pltpu.SemaphoreType.DMA((2, 4)),
            pltpu.SemaphoreType.DMA((STEPS,)),
            pltpu.SemaphoreType.DMA,
        ],
        flops=2 * 512 * 4096 * (1024 + 768),
        limit=40,
    )
    theirs = [swap_core(piece) for piece in turned]
    high, low, own, other = call(
        score_kernel,
        "score_rows",
        [((512, 768), BF16)] * 4,
        (core, pred, observed),
        "smm",
        "hhmm",
        [pltpu.VMEM((32, 16, 768), F32)] * 2 + [pltpu.VMEM((512, 768), BF16)] * 2 + [pltpu.SemaphoreType.DMA((2,))],
        flops=2 * 512 * 4096 * 1024,
        limit=16,
    )
    got = swap_core(other)
    came = []
    for part in range(3):
        (send,) = make_outer((part,), 1, chips, turned, theirs, own, got)
        came.append(swap_stage(send, part, 0))
    keep = make_outer((0, 1, 2), 0, chips, turned, theirs, own, got)
    begun = make_back(0, high, low, w_out, w_in, slope)
    *came, begun = lax.optimization_barrier((*came, begun))

    send = [keep[part][1024:] + came[part][1024:] for part in range(3)]
    after = [swap_stage(send[part], part, 1) for part in range(3)]
    keep = [keep[part][:1024] + came[part][:1024] for part in range(3)]
    latent = make_back(STEPS // 2, high, low, w_out, w_in, slope, begun, cond, gain)
    *came, latent = lax.optimization_barrier((*after, latent))

    send = [keep[part][512:] + came[part][512:] for part in range(3)]
    after = [swap_stage(send[part], part, 2) for part in range(3)]
    keep = [keep[part][:512] + came[part][:512] for part in range(3)]
    beside = swap_core(latent)
    (packed,) = call(
        pack_kernel, "pack", [((8, 224, 128), F32)], (*keep, *after, latent, beside), "mmmmmmmm", "m"
    )
    got = lax.all_to_all(
        packed, AXES, split_axis=0, concat_axis=0, tiled=True, axis_index_groups=last_groups()
    )
    mine, give, latent = call(
        sum_kernel, "sum_blocks", [((96, 128), F32), ((224, 128), F32), ((128, 128), F32)], (core, got), "sm", "mmm"
    )
    given = swap_core(give)
    return tuple(
        call(
            place_kernel,
            "place_blocks",
            [((32, 768), F32), ((128, 128), F32)],
            (core, mine, given, latent),
            "smmm",
            "mm",
        )
    )


def solution(mesh):
    placed = (
        P("token", "member"),
        P("member", "token", None),
        P(),
        P(),
        P(),
        P(),
        P(("token", "member"), None),
    )
    return jax.shard_map(
        per_device,
        mesh=mesh,
        in_specs=placed,
        out_specs=(P(("member", "token"), None), P("token", "member")),
        check_vma=False,
    )
```

```python
import functools

import jax
import jax.numpy as jnp
import numpy as np
from jax import lax
from jax.experimental import pallas as pl
from jax.experimental.pallas import tpu as pltpu
from jax.sharding import PartitionSpec as P

AXES = ("member", "token")
FIRST = (("x0", "x1", "z1"), ("y0", "y1", "z0"))
CHUNK = 512
STEPS = 4096 // CHUNK
F32, BF16 = jnp.float32, jnp.bfloat16
LAST = (((1,), (1,)), ((), ()))


def coords(index):
    member, token = divmod(index, 16)
    y, z_lo = divmod(member, 2)
    z_hi, x, core = token // 8, token // 2 % 4, token % 2
    return {"x": x, "y": y, "z": 2 * z_hi + z_lo}, core


def index_of(place, core):
    return (place["y"] * 2 + place["z"] % 2) * 16 + (place["z"] // 2) * 8 + place["x"] * 2 + core


def order_of(core, part):
    return FIRST[core][part:] + FIRST[core][:part]


def group_place(index):
    place, core = coords(index)
    if core == 0:
        return (0, place["x"], place["z"] // 2), place["y"] * 2 + place["z"] % 2
    return (1, place["y"], place["z"] % 2 ^ place["z"] // 2), place["z"] // 2 * 4 + place["x"]


def last_groups():
    groups = {}
    for index in range(128):
        group, at = group_place(index)
        groups.setdefault(group, [None] * 8)[at] = index
    return [groups[name] for name in sorted(groups)]


def shift_of(core, part, group):
    bits = {dim: group >> (2 - at) & 1 for at, dim in enumerate(order_of(core, part))}
    if core == 0:
        return bits["z1"] * 4 + bits["x1"] * 2 + (bits["x0"] ^ bits["x1"])
    return (bits["y1"] * 2 + (bits["y0"] ^ bits["y1"])) * 16 + bits["z0"] * 8


def chip_at(device, part, place):
    group, at = divmod(place, 8)
    chip = device // 2
    low = at * 8 + ((chip & 7) ^ shift_of(0, part, group))
    lean = (chip >> 3 ^ chip >> 2) & 1
    line = ((chip & 48) + lean * 8) ^ (shift_of(1, part, group) ^ (at >> 2) * 8)
    return jnp.where(device % 2 == 0, low, line + at)


def partner(index, dim):
    place, core = coords(index)
    place[dim[0]] ^= 1 if dim[1] == "0" else 3
    return index_of(place, core)


def swap_stage(values, part, stage):
    pairs = [(i, partner(i, order_of(i % 2, part)[stage])) for i in range(128)]
    return lax.ppermute(values, AXES, pairs)


def swap_core(values):
    return lax.ppermute(values, AXES, [(i, i ^ 1) for i in range(128)])


def call(body, name, outs, args, spaces, out_spaces, scratch=(), flops=0, limit=16):
    placed = [
        pltpu.with_memory_space_constraint(a, {"v": pltpu.VMEM, "a": pltpu.HBM}[space]) if space in "va" else a
        for a, space in zip(args, spaces)
    ]
    kinds = {"s": pltpu.SMEM, "v": pltpu.VMEM, "m": pltpu.VMEM, "a": pltpu.HBM, "h": pltpu.HBM}
    return pl.pallas_call(
        body,
        in_specs=[pl.BlockSpec(memory_space=kinds[space]) for space in spaces],
        out_specs=[pl.BlockSpec(memory_space=kinds[space]) for space in out_spaces],
        out_shape=[
            {"v": pltpu.VMEM, "h": pltpu.HBM, "m": jax.ShapeDtypeStruct}[space](shape, kind)
            for (shape, kind), space in zip(outs, out_spaces)
        ],
        scratch_shapes=list(scratch),
        compiler_params=pltpu.CompilerParams(vmem_limit_bytes=limit * 1024 * 1024),
        cost_estimate=pl.CostEstimate(
            flops=flops, bytes_accessed=sum(a.size * a.dtype.itemsize for a in args), transcendentals=0
        ),
        name=name,
    )(*placed)


def gather_kernel(noise_hbm, latents_hbm, out_ref, noise_ref, latents_ref, sems):
    copies = [
        pltpu.make_async_copy(noise_hbm, noise_ref, sems.at[0]),
        pltpu.make_async_copy(latents_hbm, latents_ref, sems.at[1]),
    ]
    for copy in copies:
        copy.start()
    for copy in copies:
        copy.wait()
    for j in range(8):
        rows = slice(j * 16, j * 16 + 16)
        for i in range(4):
            out_ref[j, i] = noise_ref[i, rows, :]
        out_ref[j, 4] = latents_ref[rows, :]


def forward_kernel(moved_ref, nw_hbm, gain_ref, w_in_hbm, w_out_hbm, cond_hbm, slope_hbm, pred_ref, *rest):
    turned = rest[:4]
    cond_ref, slope_ref, pre_ref, total_ref, out_sems, cond_sem = rest[4:10]
    w_in_ref, w_out_ref, nw_ref, in_sems, mid_sems, nw_sem = rest[10:]

    def columns(step):
        return slice(step * CHUNK, (step + 1) * CHUNK)

    def put(step):
        return pltpu.make_async_copy(slope_ref.at[step], slope_hbm.at[step], out_sems.at[step])

    def fetch_in(i):
        rows = slice(i * 128, i * 128 + 128)
        return pltpu.make_async_copy(w_in_hbm.at[rows, :], w_in_ref.at[rows, :], in_sems.at[i])

    def fetch_out(step):
        return pltpu.make_async_copy(w_out_hbm.at[columns(step), :], w_out_ref.at[columns(step), :], mid_sems.at[step])

    fetch_nw = pltpu.make_async_copy(nw_hbm, nw_ref, nw_sem)
    fetch_nw.start()
    for i in range(8):
        fetch_in(i).start()
    for step in range(STEPS):
        fetch_out(step).start()
    moved = moved_ref[...]
    noise = moved[:, :4].reshape(512, 128)
    latents = jnp.concatenate([moved[j, 4] for j in range(8)], axis=1).astype(F32)
    fetch_nw.wait()
    cond = jnp.dot(noise, nw_ref[...], preferred_element_type=F32)
    cond = (cond.reshape(32, 16, 1024) + latents[None]).reshape(512, 1024)
    scale = lax.rsqrt(jnp.mean(cond * cond, axis=-1, keepdims=True) + 1e-05)
    cond_ref[...] = cond
    put_cond = pltpu.make_async_copy(cond_ref, cond_hbm, cond_sem)
    put_cond.start()
    normed = (cond * scale * gain_ref[...].astype(F32)).astype(BF16)
    root = np.float32(np.sqrt(2 / np.pi))
    cubic = np.float32(np.sqrt(2 / np.pi) * 0.044715)
    for step in range(STEPS + 1):
        if step == 0:
            for i in range(8):
                fetch_in(i).wait()
        if step < STEPS:
            pre_ref[step % 2] = jnp.dot(normed, w_in_ref[:, columns(step)], preferred_element_type=F32)
        if step == 1:
            for i in range(STEPS):
                fetch_out(i).wait()
        if step > 0:
            done = step - 1
            pre = pre_ref[done % 2]
            square = pre * pre
            bend = jnp.tanh(pre * (root + cubic * square))
            cdf = 0.5 + 0.5 * bend
            value = pre * cdf
            hidden = value.astype(BF16)
            slope_ref[done] = cdf + (value - value * cdf) * (2.0 * root + 6.0 * cubic * square)
            flipped = hidden.T.reshape(8, 4, 16, 512)
            for i in range(4):
                turned[i][done * 128 : done * 128 + 128, :] = flipped[:, i].reshape(128, 512)
            put(done).start()
            term = jnp.dot(hidden, w_out_ref[columns(done), :], preferred_element_type=F32)
            if done == 0:
                total_ref[...] = term
            elif done < STEPS - 1:
                total_ref[...] += term
            else:
                pred_ref[...] = (total_ref[...] + term).astype(BF16)
    put_cond.wait()
    for step in range(STEPS):
        put(step).wait()


def score_kernel(core_ref, pred_in_ref, target_ref, high_hbm, low_hbm, own_ref, other_ref, pred_ref, grad_ref, high_ref, low_ref, sems):
    pred_ref[...] = pred_in_ref[...].astype(F32).reshape(32, 16, 768)
    grad_ref[...] = jnp.zeros_like(grad_ref)

    for member in range(32):
        own = pred_ref[member]
        total = jnp.zeros((16, 768), F32)
        for offset in range(1, 17 if member < 16 else 16):
            other = (member + offset) % 32
            diff = own - pred_ref[other]
            push = diff * lax.rsqrt(jnp.mean(diff * diff, axis=-1, keepdims=True) + 1e-06)
            grad_ref[other] -= push
            total = total + push
        grad_ref[member] += total
    err = pred_ref[...] - target_ref[...].astype(F32)[None]
    inverse = lax.rsqrt(jnp.mean(err * err, axis=-1, keepdims=True) + 1e-06)
    grad = (err * inverse - grad_ref[...] * (1.0 / 32)).reshape(512, 768)
    high = grad.astype(BF16)
    low = (grad - high.astype(F32)).astype(BF16)
    high_ref[...] = high
    low_ref[...] = low
    copies = [
        pltpu.make_async_copy(high_ref, high_hbm, sems.at[0]),
        pltpu.make_async_copy(low_ref, low_hbm, sems.at[1]),
    ]
    for copy in copies:
        copy.start()

    def halves(mine_ref, yours_ref):
        for part in range(3):
            at = part * 128
            mine_ref[:, 2 * at : 2 * at + 128] = high[:, at : at + 128]
            mine_ref[:, 2 * at + 128 : 2 * at + 256] = low[:, at : at + 128]
            yours_ref[:, 2 * at : 2 * at + 128] = high[:, 384 + at : 512 + at]
            yours_ref[:, 2 * at + 128 : 2 * at + 256] = low[:, 384 + at : 512 + at]

    @pl.when(core_ref[0] == 0)
    def _():
        halves(own_ref, other_ref)

    @pl.when(core_ref[0] == 1)
    def _():
        halves(other_ref, own_ref)

    for copy in copies:
        copy.wait()


def outer_kernel(parts, side, device_ref, own_ref, got_ref, *rest):
    mine, theirs, rest = rest[:4], rest[4:8], rest[8:]
    outs, (a_ref, b_ref) = rest[: len(parts)], rest[len(parts) :]
    for slot, part in enumerate(parts):
        fields = slice(part * 256, part * 256 + 256)
        for quarter in range(4):
            at = slice(quarter * 512, quarter * 512 + 512)
            for block in range(8):
                chip = chip_at(device_ref[0], part, side * 32 + quarter * 8 + block)
                rows = pl.ds(pl.multiple_of(chip * 16, 16), 16)
                for i in range(4):
                    first = quarter * 512 + block * 64 + i * 16
                    a_ref[first : first + 16, :] = mine[i][rows, :]
                    b_ref[first : first + 16, :] = theirs[i][rows, :]
            both = jnp.dot(a_ref[at, :], own_ref[:, fields], preferred_element_type=F32)
            both += jnp.dot(b_ref[at, :], got_ref[:, fields], preferred_element_type=F32)
            outs[slot][at, :] = both[:, :128] + both[:, 128:]


def make_outer(parts, side, device, mine, theirs, own, got):
    n = len(parts)
    return call(
        functools.partial(outer_kernel, parts, side),
        "outer_send" if side else "outer_keep",
        [((2048, 128), F32)] * n,
        (device, own, got, *mine, *theirs),
        "smm" + "m" * 8,
        "m" * n,
        [pltpu.VMEM((2048, 512), BF16)] * 2,
        flops=2 * 1024 * 256 * 2048 * n,
        limit=8,
    )


def back_kernel(begin, high_ref, low_ref, w_out_ref, w_in_ref, slope_ref, *rest):
    if begin == 0:
        (total_ref,) = rest
    else:
        before_ref, cond_ref, gain_ref, out_ref, total_ref = rest
    for step in range(begin, begin + STEPS // 2):
        columns = slice(step * CHUNK, (step + 1) * CHUNK)
        w_out = w_out_ref[columns, :]
        back = lax.dot_general(high_ref[...], w_out, LAST, preferred_element_type=F32)
        back += lax.dot_general(low_ref[...], w_out, LAST, preferred_element_type=F32)
        dpre = (back * slope_ref[step]).astype(BF16)
        term = lax.dot_general(dpre, w_in_ref[:, columns], LAST, preferred_element_type=F32)
        if step == 0:
            total_ref[...] = term
        elif step == begin:
            total_ref[...] = before_ref[...] + term
        else:
            total_ref[...] += term
    if begin == 0:
        return
    cond = cond_ref[...]
    scale = lax.rsqrt(jnp.mean(cond * cond, axis=-1, keepdims=True) + 1e-05)
    weighted = total_ref[...] * gain_ref[...].astype(F32)
    mean = jnp.mean(weighted * cond, axis=-1, keepdims=True)
    dcond = scale * weighted - cond * (scale * scale * scale * mean)
    total = jnp.sum(dcond.reshape(32, 16, 1024), axis=0)
    for j in range(8):
        out_ref[j] = total[:, j * 128 : j * 128 + 128]


def make_back(begin, high, low, w_out, w_in, slope, *more):
    (out,) = call(
        functools.partial(back_kernel, begin),
        "back_end" if begin else "back_begin",
        [((8, 16, 128) if begin else (512, 1024), F32)],
        (high, low, w_out, w_in, slope) + more,
        "m" * (5 + len(more)),
        "m",
        [pltpu.VMEM((512, 1024), F32)] if begin else [],
        flops=512 * 4096 * (768 * 2 + 1024),
        limit=10,
    )
    return out


def pack_kernel(*refs):
    keep, came, (mine_ref, theirs_ref, out_ref) = refs[:3], refs[3:6], refs[6:]
    for part in range(3):
        for j in range(8):
            rows = slice(j * 64, j * 64 + 64)
            out_ref[j, part * 64 : part * 64 + 64, :] = keep[part][rows, :] + came[part][rows, :]
    out_ref[:, 192:208, :] = mine_ref[...]
    out_ref[:, 208:224, :] = theirs_ref[...]


def sum_kernel(core_ref, got_ref, mine_ref, give_ref, latent_ref):
    total = got_ref[0, :192, :]
    for j in range(1, 8):
        total += got_ref[j, :192, :]
    latent_ref[...] = got_ref[:, 192:208, :].reshape(128, 128)
    give_ref[96:, :] = got_ref[:, 208:224, :].reshape(128, 128)
    low = core_ref[0] == 0
    for part in range(3):
        top = total[part * 64 : part * 64 + 32]
        bottom = total[part * 64 + 32 : part * 64 + 64]
        mine_ref[part * 32 : part * 32 + 32, :] = jnp.where(low, top, bottom)
        give_ref[part * 32 : part * 32 + 32, :] = jnp.where(low, bottom, top)


def place_kernel(core_ref, mine_ref, given_ref, latent_ref, grad_ref, out_ref):
    low = core_ref[0] == 0
    for part in range(3):
        mine = mine_ref[part * 32 : part * 32 + 32, :]
        given = given_ref[part * 32 : part * 32 + 32, :]
        grad_ref[:, part * 128 : part * 128 + 128] = jnp.where(low, mine, given)
        grad_ref[:, 384 + part * 128 : 512 + part * 128] = jnp.where(low, given, mine)
    out_ref[...] = jnp.where(low, latent_ref[...], given_ref[96:, :])


def per_device(latents, noise, noise_weight, gain, w_in, w_out, observed):
    device = lax.axis_index(AXES)
    core = (device % 2).reshape(1)
    device = device.reshape(1)
    gain = gain.reshape(1, 1024)

    noise, latents, device, core = lax.optimization_barrier((noise, latents, device, core))
    (moved,) = call(gather_kernel, "gather_in", [((8, 5, 16, 128), BF16)], (noise, latents), "aa", "m", [pltpu.VMEM((4, 128, 128), BF16), pltpu.VMEM((128, 128), BF16), pltpu.SemaphoreType.DMA((2,))])
    moved = lax.all_to_all(moved, "member", split_axis=0, concat_axis=0, tiled=True)
    cond, slope, pred, *turned = call(
        forward_kernel,
        "forward_rows",
        [((512, 1024), F32), ((STEPS, 512, CHUNK), F32), ((512, 768), BF16)] + [((1024, 512), BF16)] * 4,
        (moved, noise_weight, gain, w_in, w_out),
        "mamaa",
        "hhmmmmm",
        [
            pltpu.VMEM((512, 1024), F32),
            pltpu.VMEM((STEPS, 512, CHUNK), F32),
            pltpu.VMEM((2, 512, CHUNK), F32),
            pltpu.VMEM((512, 768), F32),
            pltpu.SemaphoreType.DMA((STEPS,)),
            pltpu.SemaphoreType.DMA,
            pltpu.VMEM((1024, 4096), BF16),
            pltpu.VMEM((4096, 768), BF16),
            pltpu.VMEM((128, 1024), BF16),
            pltpu.SemaphoreType.DMA((8,)),
            pltpu.SemaphoreType.DMA((STEPS,)),
            pltpu.SemaphoreType.DMA,
        ],
        flops=2 * 512 * 4096 * (1024 + 768),
        limit=40,
    )
    theirs = [swap_core(piece) for piece in turned]
    high, low, own, other = call(
        score_kernel,
        "score_rows",
        [((512, 768), BF16)] * 4,
        (core, pred, observed),
        "smm",
        "hhmm",
        [pltpu.VMEM((32, 16, 768), F32)] * 2 + [pltpu.VMEM((512, 768), BF16)] * 2 + [pltpu.SemaphoreType.DMA((2,))],
        flops=2 * 512 * 4096 * 1024,
        limit=16,
    )
    got = swap_core(other)
    came = []
    for part in range(3):
        (send,) = make_outer((part,), 1, device, turned, theirs, own, got)
        came.append(swap_stage(send, part, 0))
    keep = make_outer((0, 1, 2), 0, device, turned, theirs, own, got)
    begun = make_back(0, high, low, w_out, w_in, slope)
    *came, begun = lax.optimization_barrier((*came, begun))

    send = [keep[part][1024:] + came[part][1024:] for part in range(3)]
    after = [swap_stage(send[part], part, 1) for part in range(3)]
    keep = [keep[part][:1024] + came[part][:1024] for part in range(3)]
    latent = make_back(STEPS // 2, high, low, w_out, w_in, slope, begun, cond, gain)
    *came, latent = lax.optimization_barrier((*after, latent))

    send = [keep[part][512:] + came[part][512:] for part in range(3)]
    after = [swap_stage(send[part], part, 2) for part in range(3)]
    keep = [keep[part][:512] + came[part][:512] for part in range(3)]
    beside = swap_core(latent)
    (packed,) = call(
        pack_kernel, "pack", [((8, 224, 128), F32)], (*keep, *after, latent, beside), "mmmmmmmm", "m"
    )
    got = lax.all_to_all(
        packed, AXES, split_axis=0, concat_axis=0, tiled=True, axis_index_groups=last_groups()
    )
    mine, give, latent = call(
        sum_kernel, "sum_blocks", [((96, 128), F32), ((224, 128), F32), ((128, 128), F32)], (core, got), "sm", "mmm"
    )
    given = swap_core(give)
    return tuple(
        call(
            place_kernel,
            "place_blocks",
            [((32, 768), F32), ((128, 128), F32)],
            (core, mine, given, latent),
            "smmm",
            "mm",
        )
    )


def solution(mesh):
    placed = (
        P("token", "member"),
        P("member", "token", None),
        P(),
        P(),
        P(),
        P(),
        P(("token", "member"), None),
    )
    return jax.shard_map(
        per_device,
        mesh=mesh,
        in_specs=placed,
        out_specs=(P(("member", "token"), None), P("token", "member")),
        check_vma=False,
    )
```

```python
import functools

import jax
import jax.numpy as jnp
import numpy as np
from jax import lax
from jax.experimental import pallas as pl
from jax.experimental.pallas import tpu as pltpu
from jax.sharding import PartitionSpec as P

AXES = ("member", "token")
FIRST = (("x0", "x1", "z1"), ("y0", "y1", "z0"))
CHUNK = 512
STEPS = 4096 // CHUNK
F32, BF16 = jnp.float32, jnp.bfloat16
LAST = (((1,), (1,)), ((), ()))


def coords(index):
    member, token = divmod(index, 16)
    y, z_lo = divmod(member, 2)
    z_hi, x, core = token // 8, token // 2 % 4, token % 2
    return {"x": x, "y": y, "z": 2 * z_hi + z_lo}, core


def index_of(place, core):
    return (place["y"] * 2 + place["z"] % 2) * 16 + (place["z"] // 2) * 8 + place["x"] * 2 + core


def order_of(core, part):
    return FIRST[core][part:] + FIRST[core][:part]


def group_place(index):
    place, core = coords(index)
    if core == 0:
        return (0, place["x"], place["z"] // 2), place["y"] * 2 + place["z"] % 2
    return (1, place["y"], place["z"] % 2 ^ place["z"] // 2), place["z"] // 2 * 4 + place["x"]


def last_groups():
    groups = {}
    for index in range(128):
        group, at = group_place(index)
        groups.setdefault(group, [None] * 8)[at] = index
    return [groups[name] for name in sorted(groups)]


def shift_of(core, part, group):
    bits = {dim: group >> (2 - at) & 1 for at, dim in enumerate(order_of(core, part))}
    if core == 0:
        return bits["z1"] * 4 + bits["x1"] * 2 + (bits["x0"] ^ bits["x1"])
    return (bits["y1"] * 2 + (bits["y0"] ^ bits["y1"])) * 16 + bits["z0"] * 8


def chip_at(device, part, place):
    group, at = divmod(place, 8)
    chip = device // 2
    low = at * 8 + ((chip & 7) ^ shift_of(0, part, group))
    lean = (chip >> 3 ^ chip >> 2) & 1
    line = ((chip & 48) + lean * 8) ^ (shift_of(1, part, group) ^ (at >> 2) * 8)
    return jnp.where(device % 2 == 0, low, line + at)


def partner(index, dim):
    place, core = coords(index)
    place[dim[0]] ^= 1 if dim[1] == "0" else 3
    return index_of(place, core)


def swap_stage(values, part, stage):
    pairs = [(i, partner(i, order_of(i % 2, part)[stage])) for i in range(128)]
    return lax.ppermute(values, AXES, pairs)


def swap_core(values):
    return lax.ppermute(values, AXES, [(i, i ^ 1) for i in range(128)])


def call(body, name, outs, args, spaces, out_spaces, scratch=(), flops=0, limit=16):
    placed = [
        pltpu.with_memory_space_constraint(a, {"v": pltpu.VMEM, "a": pltpu.HBM}[space]) if space in "va" else a
        for a, space in zip(args, spaces)
    ]
    kinds = {"s": pltpu.SMEM, "v": pltpu.VMEM, "m": pltpu.VMEM, "a": pltpu.HBM, "h": pltpu.HBM}
    return pl.pallas_call(
        body,
        in_specs=[pl.BlockSpec(memory_space=kinds[space]) for space in spaces],
        out_specs=[pl.BlockSpec(memory_space=kinds[space]) for space in out_spaces],
        out_shape=[
            {"v": pltpu.VMEM, "h": pltpu.HBM, "m": jax.ShapeDtypeStruct}[space](shape, kind)
            for (shape, kind), space in zip(outs, out_spaces)
        ],
        scratch_shapes=list(scratch),
        compiler_params=pltpu.CompilerParams(vmem_limit_bytes=limit * 1024 * 1024),
        cost_estimate=pl.CostEstimate(
            flops=flops, bytes_accessed=sum(a.size * a.dtype.itemsize for a in args), transcendentals=0
        ),
        name=name,
    )(*placed)


def gather_kernel(noise_hbm, latents_hbm, out_ref, noise_ref, latents_ref, sems):
    copies = [
        pltpu.make_async_copy(noise_hbm, noise_ref, sems.at[0]),
        pltpu.make_async_copy(latents_hbm, latents_ref, sems.at[1]),
    ]
    for copy in copies:
        copy.start()
    for copy in copies:
        copy.wait()
    for j in range(8):
        rows = slice(j * 16, j * 16 + 16)
        for i in range(4):
            out_ref[j, i] = noise_ref[i, rows, :]
        out_ref[j, 4] = latents_ref[rows, :]


def forward_kernel(moved_ref, nw_hbm, gain_ref, w_in_hbm, w_out_hbm, cond_hbm, slope_hbm, pred_ref, *rest):
    turned = rest[:4]
    cond_ref, slope_ref, pre_ref, total_ref, out_sems, cond_sem = rest[4:10]
    w_in_ref, w_out_ref, nw_ref, in_sems, mid_sems, nw_sem = rest[10:]

    def columns(step):
        return slice(step * CHUNK, (step + 1) * CHUNK)

    def put(step):
        return pltpu.make_async_copy(slope_ref.at[step], slope_hbm.at[step], out_sems.at[step])

    def fetch_in(i):
        rows = slice(i * 128, i * 128 + 128)
        return pltpu.make_async_copy(w_in_hbm.at[rows, :], w_in_ref.at[rows, :], in_sems.at[i])

    def fetch_out(step):
        return pltpu.make_async_copy(w_out_hbm.at[columns(step), :], w_out_ref.at[columns(step), :], mid_sems.at[step])

    fetch_nw = pltpu.make_async_copy(nw_hbm, nw_ref, nw_sem)
    fetch_nw.start()
    for i in range(8):
        fetch_in(i).start()
    for step in range(STEPS):
        fetch_out(step).start()
    moved = moved_ref[...]
    noise = moved[:, :4].reshape(512, 128)
    latents = jnp.concatenate([moved[j, 4] for j in range(8)], axis=1).astype(F32)
    fetch_nw.wait()
    cond = jnp.dot(noise, nw_ref[...], preferred_element_type=F32)
    cond = (cond.reshape(32, 16, 1024) + latents[None]).reshape(512, 1024)
    scale = lax.rsqrt(jnp.mean(cond * cond, axis=-1, keepdims=True) + 1e-05)
    cond_ref[...] = cond
    put_cond = pltpu.make_async_copy(cond_ref, cond_hbm, cond_sem)
    put_cond.start()
    normed = (cond * scale * gain_ref[...].astype(F32)).astype(BF16)
    root = np.float32(np.sqrt(2 / np.pi))
    cubic = np.float32(np.sqrt(2 / np.pi) * 0.044715)
    for step in range(STEPS + 1):
        if step == 0:
            for i in range(8):
                fetch_in(i).wait()
        if step < STEPS:
            pre_ref[step % 2] = jnp.dot(normed, w_in_ref[:, columns(step)], preferred_element_type=F32)
        if step == 1:
            for i in range(STEPS):
                fetch_out(i).wait()
        if step > 0:
            done = step - 1
            pre = pre_ref[done % 2]
            square = pre * pre
            bend = jnp.tanh(pre * (root + cubic * square))
            cdf = 0.5 + 0.5 * bend
            value = pre * cdf
            hidden = value.astype(BF16)
            slope_ref[done] = cdf + (value - value * cdf) * (2.0 * root + 6.0 * cubic * square)
            flipped = hidden.T.reshape(8, 4, 16, 512)
            for i in range(4):
                turned[i][done * 128 : done * 128 + 128, :] = flipped[:, i].reshape(128, 512)
            put(done).start()
            term = jnp.dot(hidden, w_out_ref[columns(done), :], preferred_element_type=F32)
            if done == 0:
                total_ref[...] = term
            elif done < STEPS - 1:
                total_ref[...] += term
            else:
                pred_ref[...] = (total_ref[...] + term).astype(BF16)
    put_cond.wait()
    for step in range(STEPS):
        put(step).wait()


def score_kernel(core_ref, pred_in_ref, target_ref, high_hbm, low_hbm, own_ref, other_ref, pred_ref, grad_ref, high_ref, low_ref, sems):
    pred_ref[...] = pred_in_ref[...].astype(F32).reshape(32, 16, 768)
    grad_ref[...] = jnp.zeros_like(grad_ref)

    for member in range(32):
        own = pred_ref[member]
        total = jnp.zeros((16, 768), F32)
        for offset in range(1, 17 if member < 16 else 16):
            other = (member + offset) % 32
            diff = own - pred_ref[other]
            push = diff * lax.rsqrt(jnp.mean(diff * diff, axis=-1, keepdims=True) + 1e-06)
            grad_ref[other] -= push
            total = total + push
        grad_ref[member] += total
    err = pred_ref[...] - target_ref[...].astype(F32)[None]
    inverse = lax.rsqrt(jnp.mean(err * err, axis=-1, keepdims=True) + 1e-06)
    grad = (err * inverse - grad_ref[...] * (1.0 / 32)).reshape(512, 768)
    high = grad.astype(BF16)
    low = (grad - high.astype(F32)).astype(BF16)
    high_ref[...] = high
    low_ref[...] = low
    copies = [
        pltpu.make_async_copy(high_ref, high_hbm, sems.at[0]),
        pltpu.make_async_copy(low_ref, low_hbm, sems.at[1]),
    ]
    for copy in copies:
        copy.start()

    def halves(mine_ref, yours_ref):
        for part in range(3):
            at = part * 128
            mine_ref[:, 2 * at : 2 * at + 128] = high[:, at : at + 128]
            mine_ref[:, 2 * at + 128 : 2 * at + 256] = low[:, at : at + 128]
            yours_ref[:, 2 * at : 2 * at + 128] = high[:, 384 + at : 512 + at]
            yours_ref[:, 2 * at + 128 : 2 * at + 256] = low[:, 384 + at : 512 + at]

    @pl.when(core_ref[0] == 0)
    def _():
        halves(own_ref, other_ref)

    @pl.when(core_ref[0] == 1)
    def _():
        halves(other_ref, own_ref)

    for copy in copies:
        copy.wait()


def outer_kernel(side, sources, added, device_ref, *refs):
    grads, refs = refs[:sources], refs[sources:]
    turned, refs = [refs[4 * i : 4 * i + 4] for i in range(sources)], refs[4 * sources :]
    before, refs = refs[: 3 * added], refs[3 * added :]
    outs, rows_refs = refs[:3], refs[3:]
    for part in range(3):
        fields = slice(part * 256, part * 256 + 256)
        for quarter in range(4):
            at = slice(quarter * 512, quarter * 512 + 512)
            for block in range(8):
                chip = chip_at(device_ref[0], part, side * 32 + quarter * 8 + block)
                rows = pl.ds(pl.multiple_of(chip * 16, 16), 16)
                for i in range(4):
                    first = quarter * 512 + block * 64 + i * 16
                    for source in range(sources):
                        rows_refs[source][first : first + 16, :] = turned[source][i][rows, :]
            both = jnp.dot(rows_refs[0][at, :], grads[0][:, fields], preferred_element_type=F32)
            for source in range(1, sources):
                both += jnp.dot(rows_refs[source][at, :], grads[source][:, fields], preferred_element_type=F32)
            total = both[:, :128] + both[:, 128:]
            outs[part][at, :] = total + before[part][at, :] if added else total


def make_outer(name, side, device, grads, turned, before=()):
    n = len(grads)
    pieces = [piece for pieces in turned for piece in pieces]
    return call(
        functools.partial(outer_kernel, side, n, len(before) // 3),
        name,
        [((2048, 128), F32)] * 3,
        (device, *grads, *pieces, *before),
        "s" + "m" * (5 * n + len(before)),
        "mmm",
        [pltpu.VMEM((2048, 512), BF16)] * n,
        flops=2 * 512 * n * 256 * 2048 * 3,
        limit=8,
    )


def back_kernel(begin, high_ref, low_ref, w_out_ref, w_in_ref, slope_ref, *rest):
    if begin == 0:
        (total_ref,) = rest
    else:
        before_ref, cond_ref, gain_ref, out_ref, total_ref = rest
    for step in range(begin, begin + STEPS // 2):
        columns = slice(step * CHUNK, (step + 1) * CHUNK)
        w_out = w_out_ref[columns, :]
        back = lax.dot_general(high_ref[...], w_out, LAST, preferred_element_type=F32)
        back += lax.dot_general(low_ref[...], w_out, LAST, preferred_element_type=F32)
        dpre = (back * slope_ref[step]).astype(BF16)
        term = lax.dot_general(dpre, w_in_ref[:, columns], LAST, preferred_element_type=F32)
        if step == 0:
            total_ref[...] = term
        elif step == begin:
            total_ref[...] = before_ref[...] + term
        else:
            total_ref[...] += term
    if begin == 0:
        return
    cond = cond_ref[...]
    scale = lax.rsqrt(jnp.mean(cond * cond, axis=-1, keepdims=True) + 1e-05)
    weighted = total_ref[...] * gain_ref[...].astype(F32)
    mean = jnp.mean(weighted * cond, axis=-1, keepdims=True)
    dcond = scale * weighted - cond * (scale * scale * scale * mean)
    total = jnp.sum(dcond.reshape(32, 16, 1024), axis=0)
    for j in range(8):
        out_ref[j] = total[:, j * 128 : j * 128 + 128]


def make_back(begin, high, low, w_out, w_in, slope, *more):
    (out,) = call(
        functools.partial(back_kernel, begin),
        "back_end" if begin else "back_begin",
        [((8, 16, 128) if begin else (512, 1024), F32)],
        (high, low, w_out, w_in, slope) + more,
        "m" * (5 + len(more)),
        "m",
        [pltpu.VMEM((512, 1024), F32)] if begin else [],
        flops=512 * 4096 * (768 * 2 + 1024),
        limit=10,
    )
    return out


def pack_kernel(*refs):
    keep, came, (mine_ref, theirs_ref, out_ref) = refs[:3], refs[3:6], refs[6:]
    for part in range(3):
        for j in range(8):
            rows = slice(j * 64, j * 64 + 64)
            out_ref[j, part * 64 : part * 64 + 64, :] = keep[part][rows, :] + came[part][rows, :]
    out_ref[:, 192:208, :] = mine_ref[...]
    out_ref[:, 208:224, :] = theirs_ref[...]


def sum_kernel(core_ref, got_ref, mine_ref, give_ref, latent_ref):
    total = got_ref[0, :192, :]
    for j in range(1, 8):
        total += got_ref[j, :192, :]
    latent_ref[...] = got_ref[:, 192:208, :].reshape(128, 128)
    give_ref[96:, :] = got_ref[:, 208:224, :].reshape(128, 128)
    low = core_ref[0] == 0
    for part in range(3):
        top = total[part * 64 : part * 64 + 32]
        bottom = total[part * 64 + 32 : part * 64 + 64]
        mine_ref[part * 32 : part * 32 + 32, :] = jnp.where(low, top, bottom)
        give_ref[part * 32 : part * 32 + 32, :] = jnp.where(low, bottom, top)


def place_kernel(core_ref, mine_ref, given_ref, latent_ref, grad_ref, out_ref):
    low = core_ref[0] == 0
    for part in range(3):
        mine = mine_ref[part * 32 : part * 32 + 32, :]
        given = given_ref[part * 32 : part * 32 + 32, :]
        grad_ref[:, part * 128 : part * 128 + 128] = jnp.where(low, mine, given)
        grad_ref[:, 384 + part * 128 : 512 + part * 128] = jnp.where(low, given, mine)
    out_ref[...] = jnp.where(low, latent_ref[...], given_ref[96:, :])


def per_device(latents, noise, noise_weight, gain, w_in, w_out, observed):
    device = lax.axis_index(AXES)
    core = (device % 2).reshape(1)
    device = device.reshape(1)
    gain = gain.reshape(1, 1024)

    noise, latents, device, core = lax.optimization_barrier((noise, latents, device, core))
    (moved,) = call(gather_kernel, "gather_in", [((8, 5, 16, 128), BF16)], (noise, latents), "aa", "m", [pltpu.VMEM((4, 128, 128), BF16), pltpu.VMEM((128, 128), BF16), pltpu.SemaphoreType.DMA((2,))])
    moved = lax.all_to_all(moved, "member", split_axis=0, concat_axis=0, tiled=True)
    cond, slope, pred, *turned = call(
        forward_kernel,
        "forward_rows",
        [((512, 1024), F32), ((STEPS, 512, CHUNK), F32), ((512, 768), BF16)] + [((1024, 512), BF16)] * 4,
        (moved, noise_weight, gain, w_in, w_out),
        "mamaa",
        "hhmmmmm",
        [
            pltpu.VMEM((512, 1024), F32),
            pltpu.VMEM((STEPS, 512, CHUNK), F32),
            pltpu.VMEM((2, 512, CHUNK), F32),
            pltpu.VMEM((512, 768), F32),
            pltpu.SemaphoreType.DMA((STEPS,)),
            pltpu.SemaphoreType.DMA,
            pltpu.VMEM((1024, 4096), BF16),
            pltpu.VMEM((4096, 768), BF16),
            pltpu.VMEM((128, 1024), BF16),
            pltpu.SemaphoreType.DMA((8,)),
            pltpu.SemaphoreType.DMA((STEPS,)),
            pltpu.SemaphoreType.DMA,
        ],
        flops=2 * 512 * 4096 * (1024 + 768),
        limit=40,
    )
    theirs = [swap_core(piece) for piece in turned]
    high, low, own, other = call(
        score_kernel,
        "score_rows",
        [((512, 768), BF16)] * 4,
        (core, pred, observed),
        "smm",
        "hhmm",
        [pltpu.VMEM((32, 16, 768), F32)] * 2 + [pltpu.VMEM((512, 768), BF16)] * 2 + [pltpu.SemaphoreType.DMA((2,))],
        flops=2 * 512 * 4096 * 1024,
        limit=16,
    )
    got = swap_core(other)
    begun = make_outer("outer_own", 1, device, (own,), (turned,))
    send = make_outer("outer_send", 1, device, (got,), (theirs,), begun)
    came = [swap_stage(send[part], part, 0) for part in range(3)]
    keep = make_outer("outer_keep", 0, device, (own, got), (turned, theirs))
    begun = make_back(0, high, low, w_out, w_in, slope)
    *came, begun = lax.optimization_barrier((*came, begun))

    send = [keep[part][1024:] + came[part][1024:] for part in range(3)]
    after = [swap_stage(send[part], part, 1) for part in range(3)]
    keep = [keep[part][:1024] + came[part][:1024] for part in range(3)]
    latent = make_back(STEPS // 2, high, low, w_out, w_in, slope, begun, cond, gain)
    *came, latent = lax.optimization_barrier((*after, latent))

    send = [keep[part][512:] + came[part][512:] for part in range(3)]
    after = [swap_stage(send[part], part, 2) for part in range(3)]
    keep = [keep[part][:512] + came[part][:512] for part in range(3)]
    beside = swap_core(latent)
    (packed,) = call(
        pack_kernel, "pack", [((8, 224, 128), F32)], (*keep, *after, latent, beside), "mmmmmmmm", "m"
    )
    got = lax.all_to_all(
        packed, AXES, split_axis=0, concat_axis=0, tiled=True, axis_index_groups=last_groups()
    )
    mine, give, latent = call(
        sum_kernel, "sum_blocks", [((96, 128), F32), ((224, 128), F32), ((128, 128), F32)], (core, got), "sm", "mmm"
    )
    given = swap_core(give)
    return tuple(
        call(
            place_kernel,
            "place_blocks",
            [((32, 768), F32), ((128, 128), F32)],
            (core, mine, given, latent),
            "smmm",
            "mm",
        )
    )


def solution(mesh):
    placed = (
        P("token", "member"),
        P("member", "token", None),
        P(),
        P(),
        P(),
        P(),
        P(("token", "member"), None),
    )
    return jax.shard_map(
        per_device,
        mesh=mesh,
        in_specs=placed,
        out_specs=(P(("member", "token"), None), P("token", "member")),
        check_vma=False,
    )
```

```python
import functools

import jax
import jax.numpy as jnp
import numpy as np
from jax import lax
from jax.experimental import pallas as pl
from jax.experimental.pallas import tpu as pltpu
from jax.sharding import PartitionSpec as P

AXES = ("member", "token")
FIRST = (("x0", "x1", "z1"), ("y0", "y1", "z0"))
CHUNK = 512
NEAR = 1024
STEPS = 4096 // CHUNK
F32, BF16 = jnp.float32, jnp.bfloat16
LAST = (((1,), (1,)), ((), ()))


def coords(index):
    member, token = divmod(index, 16)
    y, z_lo = divmod(member, 2)
    z_hi, x, core = token // 8, token // 2 % 4, token % 2
    return {"x": x, "y": y, "z": 2 * z_hi + z_lo}, core


def index_of(place, core):
    return (place["y"] * 2 + place["z"] % 2) * 16 + (place["z"] // 2) * 8 + place["x"] * 2 + core


def order_of(core, part):
    return FIRST[core][part:] + FIRST[core][:part]


def group_place(index):
    place, core = coords(index)
    if core == 0:
        return (0, place["x"], place["z"] // 2), place["y"] * 2 + place["z"] % 2
    return (1, place["y"], place["z"] % 2 ^ place["z"] // 2), place["z"] // 2 * 4 + place["x"]


def last_groups():
    groups = {}
    for index in range(128):
        group, at = group_place(index)
        groups.setdefault(group, [None] * 8)[at] = index
    return [groups[name] for name in sorted(groups)]


def shift_of(core, part, group):
    bits = {dim: group >> (2 - at) & 1 for at, dim in enumerate(order_of(core, part))}
    if core == 0:
        return bits["z1"] * 4 + bits["x1"] * 2 + (bits["x0"] ^ bits["x1"])
    return (bits["y1"] * 2 + (bits["y0"] ^ bits["y1"])) * 16 + bits["z0"] * 8


def chip_at(device, part, place):
    group, at = divmod(place, 8)
    chip = device // 2
    low = at * 8 + ((chip & 7) ^ shift_of(0, part, group))
    lean = (chip >> 3 ^ chip >> 2) & 1
    line = ((chip & 48) + lean * 8) ^ (shift_of(1, part, group) ^ (at >> 2) * 8)
    return jnp.where(device % 2 == 0, low, line + at)


def partner(index, dim):
    place, core = coords(index)
    place[dim[0]] ^= 1 if dim[1] == "0" else 3
    return index_of(place, core)


def swap_stage(values, part, stage):
    pairs = [(i, partner(i, order_of(i % 2, part)[stage])) for i in range(128)]
    return lax.ppermute(values, AXES, pairs)


def swap_core(values):
    return lax.ppermute(values, AXES, [(i, i ^ 1) for i in range(128)])


def call(body, name, outs, args, spaces, out_spaces, scratch=(), flops=0, limit=16):
    placed = [
        pltpu.with_memory_space_constraint(a, {"v": pltpu.VMEM, "a": pltpu.HBM}[space]) if space in "va" else a
        for a, space in zip(args, spaces)
    ]
    kinds = {"s": pltpu.SMEM, "v": pltpu.VMEM, "m": pltpu.VMEM, "a": pltpu.HBM, "h": pltpu.HBM}
    return pl.pallas_call(
        body,
        in_specs=[pl.BlockSpec(memory_space=kinds[space]) for space in spaces],
        out_specs=[pl.BlockSpec(memory_space=kinds[space]) for space in out_spaces],
        out_shape=[
            {"v": pltpu.VMEM, "h": pltpu.HBM, "m": jax.ShapeDtypeStruct}[space](shape, kind)
            for (shape, kind), space in zip(outs, out_spaces)
        ],
        scratch_shapes=list(scratch),
        compiler_params=pltpu.CompilerParams(vmem_limit_bytes=limit * 1024 * 1024),
        cost_estimate=pl.CostEstimate(
            flops=flops, bytes_accessed=sum(a.size * a.dtype.itemsize for a in args), transcendentals=0
        ),
        name=name,
    )(*placed)


def gather_kernel(noise_hbm, latents_hbm, out_ref, noise_ref, latents_ref, sems):
    copies = [
        pltpu.make_async_copy(noise_hbm, noise_ref, sems.at[0]),
        pltpu.make_async_copy(latents_hbm, latents_ref, sems.at[1]),
    ]
    for copy in copies:
        copy.start()
    for copy in copies:
        copy.wait()
    for j in range(8):
        rows = slice(j * 16, j * 16 + 16)
        for i in range(4):
            out_ref[j, i] = noise_ref[i, rows, :]
        out_ref[j, 4] = latents_ref[rows, :]


def fetch_kernel(w_in_hbm, near_ref, sem):
    copy = pltpu.make_async_copy(w_in_hbm.at[:, 0:NEAR], near_ref, sem)
    copy.start()
    copy.wait()


def forward_kernel(moved_ref, near_ref, nw_hbm, gain_ref, w_in_hbm, w_out_hbm, cond_hbm, slope_hbm, pred_ref, *rest):
    turned = rest[:4]
    cond_ref, slope_ref, pre_ref, total_ref, out_sems, cond_sem = rest[4:10]
    w_in_ref, w_out_ref, nw_ref, in_sem, mid_sems, nw_sem = rest[10:]

    def columns(step):
        return slice(step * CHUNK, (step + 1) * CHUNK)

    def put(step):
        return pltpu.make_async_copy(slope_ref.at[step], slope_hbm.at[step], out_sems.at[step])

    fetch_in = pltpu.make_async_copy(w_in_hbm.at[:, NEAR:], w_in_ref, in_sem)
    fetch_out = [
        pltpu.make_async_copy(w_out_hbm.at[rows, :], w_out_ref.at[rows, :], mid_sems.at[i])
        for i, rows in enumerate((slice(0, NEAR), slice(NEAR, 4096)))
    ]
    fetch_nw = pltpu.make_async_copy(nw_hbm, nw_ref, nw_sem)
    fetch_nw.start()
    fetch_out[0].start()
    fetch_in.start()
    fetch_out[1].start()
    moved = moved_ref[...]
    noise = moved[:, :4].reshape(512, 128)
    latents = jnp.concatenate([moved[j, 4] for j in range(8)], axis=1).astype(F32)
    fetch_nw.wait()
    cond = jnp.dot(noise, nw_ref[...], preferred_element_type=F32)
    cond = (cond.reshape(32, 16, 1024) + latents[None]).reshape(512, 1024)
    scale = lax.rsqrt(jnp.mean(cond * cond, axis=-1, keepdims=True) + 1e-05)
    cond_ref[...] = cond
    put_cond = pltpu.make_async_copy(cond_ref, cond_hbm, cond_sem)
    put_cond.start()
    normed = (cond * scale * gain_ref[...].astype(F32)).astype(BF16)
    root = np.float32(np.sqrt(2 / np.pi))
    cubic = np.float32(np.sqrt(2 / np.pi) * 0.044715)
    for step in range(STEPS + 1):
        if step == NEAR // CHUNK:
            fetch_in.wait()
        if step < NEAR // CHUNK:
            pre_ref[step % 2] = jnp.dot(normed, near_ref[:, columns(step)], preferred_element_type=F32)
        elif step < STEPS:
            at = slice(step * CHUNK - NEAR, (step + 1) * CHUNK - NEAR)
            pre_ref[step % 2] = jnp.dot(normed, w_in_ref[:, at], preferred_element_type=F32)
        if step == 1:
            fetch_out[0].wait()
        if step == NEAR // CHUNK + 1:
            fetch_out[1].wait()
        if step > 0:
            done = step - 1
            pre = pre_ref[done % 2]
            square = pre * pre
            bend = jnp.tanh(pre * (root + cubic * square))
            cdf = 0.5 + 0.5 * bend
            value = pre * cdf
            hidden = value.astype(BF16)
            slope_ref[done] = cdf + (value - value * cdf) * (2.0 * root + 6.0 * cubic * square)
            flipped = hidden.T.reshape(8, 4, 16, 512)
            for i in range(4):
                turned[i][done * 128 : done * 128 + 128, :] = flipped[:, i].reshape(128, 512)
            put(done).start()
            term = jnp.dot(hidden, w_out_ref[columns(done), :], preferred_element_type=F32)
            if done == 0:
                total_ref[...] = term
            elif done < STEPS - 1:
                total_ref[...] += term
            else:
                pred_ref[...] = (total_ref[...] + term).astype(BF16)
    put_cond.wait()
    for step in range(STEPS):
        put(step).wait()


def score_kernel(core_ref, pred_in_ref, target_ref, high_hbm, low_hbm, own_ref, other_ref, pred_ref, grad_ref, high_ref, low_ref, sems):
    pred_ref[...] = pred_in_ref[...].astype(F32).reshape(32, 16, 768)
    grad_ref[...] = jnp.zeros_like(grad_ref)

    for member in range(32):
        own = pred_ref[member]
        total = jnp.zeros((16, 768), F32)
        for offset in range(1, 17 if member < 16 else 16):
            other = (member + offset) % 32
            diff = own - pred_ref[other]
            push = diff * lax.rsqrt(jnp.mean(diff * diff, axis=-1, keepdims=True) + 1e-06)
            grad_ref[other] -= push
            total = total + push
        grad_ref[member] += total
    err = pred_ref[...] - target_ref[...].astype(F32)[None]
    inverse = lax.rsqrt(jnp.mean(err * err, axis=-1, keepdims=True) + 1e-06)
    grad = (err * inverse - grad_ref[...] * (1.0 / 32)).reshape(512, 768)
    high = grad.astype(BF16)
    low = (grad - high.astype(F32)).astype(BF16)
    high_ref[...] = high
    low_ref[...] = low
    copies = [
        pltpu.make_async_copy(high_ref, high_hbm, sems.at[0]),
        pltpu.make_async_copy(low_ref, low_hbm, sems.at[1]),
    ]
    for copy in copies:
        copy.start()

    def halves(mine_ref, yours_ref):
        for part in range(3):
            at = part * 128
            mine_ref[:, 2 * at : 2 * at + 128] = high[:, at : at + 128]
            mine_ref[:, 2 * at + 128 : 2 * at + 256] = low[:, at : at + 128]
            yours_ref[:, 2 * at : 2 * at + 128] = high[:, 384 + at : 512 + at]
            yours_ref[:, 2 * at + 128 : 2 * at + 256] = low[:, 384 + at : 512 + at]

    @pl.when(core_ref[0] == 0)
    def _():
        halves(own_ref, other_ref)

    @pl.when(core_ref[0] == 1)
    def _():
        halves(other_ref, own_ref)

    for copy in copies:
        copy.wait()


def outer_kernel(side, sources, added, device_ref, *refs):
    grads, refs = refs[:sources], refs[sources:]
    turned, refs = [refs[4 * i : 4 * i + 4] for i in range(sources)], refs[4 * sources :]
    before, refs = refs[: 3 * added], refs[3 * added :]
    outs, rows_refs = refs[:3], refs[3:]
    for part in range(3):
        fields = slice(part * 256, part * 256 + 256)
        for quarter in range(4):
            at = slice(quarter * 512, quarter * 512 + 512)
            for block in range(8):
                chip = chip_at(device_ref[0], part, side * 32 + quarter * 8 + block)
                rows = pl.ds(pl.multiple_of(chip * 16, 16), 16)
                for i in range(4):
                    first = quarter * 512 + block * 64 + i * 16
                    for source in range(sources):
                        rows_refs[source][first : first + 16, :] = turned[source][i][rows, :]
            both = jnp.dot(rows_refs[0][at, :], grads[0][:, fields], preferred_element_type=F32)
            for source in range(1, sources):
                both += jnp.dot(rows_refs[source][at, :], grads[source][:, fields], preferred_element_type=F32)
            total = both[:, :128] + both[:, 128:]
            outs[part][at, :] = total + before[part][at, :] if added else total


def make_outer(name, side, device, grads, turned, before=()):
    n = len(grads)
    pieces = [piece for pieces in turned for piece in pieces]
    return call(
        functools.partial(outer_kernel, side, n, len(before) // 3),
        name,
        [((2048, 128), F32)] * 3,
        (device, *grads, *pieces, *before),
        "s" + "m" * (5 * n + len(before)),
        "mmm",
        [pltpu.VMEM((2048, 512), BF16)] * n,
        flops=2 * 512 * n * 256 * 2048 * 3,
        limit=8,
    )


def back_kernel(begin, high_ref, low_ref, w_out_ref, w_in_ref, slope_ref, *rest):
    if begin == 0:
        (total_ref,) = rest
    else:
        before_ref, cond_ref, gain_ref, out_ref, total_ref = rest
    for step in range(begin, begin + STEPS // 2):
        columns = slice(step * CHUNK, (step + 1) * CHUNK)
        w_out = w_out_ref[columns, :]
        back = lax.dot_general(high_ref[...], w_out, LAST, preferred_element_type=F32)
        back += lax.dot_general(low_ref[...], w_out, LAST, preferred_element_type=F32)
        dpre = (back * slope_ref[step]).astype(BF16)
        term = lax.dot_general(dpre, w_in_ref[:, columns], LAST, preferred_element_type=F32)
        if step == 0:
            total_ref[...] = term
        elif step == begin:
            total_ref[...] = before_ref[...] + term
        else:
            total_ref[...] += term
    if begin == 0:
        return
    cond = cond_ref[...]
    scale = lax.rsqrt(jnp.mean(cond * cond, axis=-1, keepdims=True) + 1e-05)
    weighted = total_ref[...] * gain_ref[...].astype(F32)
    mean = jnp.mean(weighted * cond, axis=-1, keepdims=True)
    dcond = scale * weighted - cond * (scale * scale * scale * mean)
    total = jnp.sum(dcond.reshape(32, 16, 1024), axis=0)
    for j in range(8):
        out_ref[j] = total[:, j * 128 : j * 128 + 128]


def make_back(begin, high, low, w_out, w_in, slope, *more):
    (out,) = call(
        functools.partial(back_kernel, begin),
        "back_end" if begin else "back_begin",
        [((8, 16, 128) if begin else (512, 1024), F32)],
        (high, low, w_out, w_in, slope) + more,
        "m" * (5 + len(more)),
        "m",
        [pltpu.VMEM((512, 1024), F32)] if begin else [],
        flops=512 * 4096 * (768 * 2 + 1024),
        limit=10,
    )
    return out


def pack_kernel(*refs):
    keep, came, (mine_ref, theirs_ref, out_ref) = refs[:3], refs[3:6], refs[6:]
    for part in range(3):
        for j in range(8):
            rows = slice(j * 64, j * 64 + 64)
            out_ref[j, part * 64 : part * 64 + 64, :] = keep[part][rows, :] + came[part][rows, :]
    out_ref[:, 192:208, :] = mine_ref[...]
    out_ref[:, 208:224, :] = theirs_ref[...]


def sum_kernel(core_ref, got_ref, mine_ref, give_ref, latent_ref):
    total = got_ref[0, :192, :]
    for j in range(1, 8):
        total += got_ref[j, :192, :]
    latent_ref[...] = got_ref[:, 192:208, :].reshape(128, 128)
    give_ref[96:, :] = got_ref[:, 208:224, :].reshape(128, 128)
    low = core_ref[0] == 0
    for part in range(3):
        top = total[part * 64 : part * 64 + 32]
        bottom = total[part * 64 + 32 : part * 64 + 64]
        mine_ref[part * 32 : part * 32 + 32, :] = jnp.where(low, top, bottom)
        give_ref[part * 32 : part * 32 + 32, :] = jnp.where(low, bottom, top)


def place_kernel(core_ref, mine_ref, given_ref, latent_ref, grad_ref, out_ref):
    low = core_ref[0] == 0
    for part in range(3):
        mine = mine_ref[part * 32 : part * 32 + 32, :]
        given = given_ref[part * 32 : part * 32 + 32, :]
        grad_ref[:, part * 128 : part * 128 + 128] = jnp.where(low, mine, given)
        grad_ref[:, 384 + part * 128 : 512 + part * 128] = jnp.where(low, given, mine)
    out_ref[...] = jnp.where(low, latent_ref[...], given_ref[96:, :])


def per_device(latents, noise, noise_weight, gain, w_in, w_out, observed):
    device = lax.axis_index(AXES)
    core = (device % 2).reshape(1)
    device = device.reshape(1)
    gain = gain.reshape(1, 1024)

    noise, latents, device, core = lax.optimization_barrier((noise, latents, device, core))
    (moved,) = call(gather_kernel, "gather_in", [((8, 5, 16, 128), BF16)], (noise, latents), "aa", "m", [pltpu.VMEM((4, 128, 128), BF16), pltpu.VMEM((128, 128), BF16), pltpu.SemaphoreType.DMA((2,))])
    moved = lax.all_to_all(moved, "member", split_axis=0, concat_axis=0, tiled=True)
    (near,) = call(
        fetch_kernel, "fetch_near", [((1024, NEAR), BF16)], (w_in,), "a", "m", [pltpu.SemaphoreType.DMA], limit=1
    )
    cond, slope, pred, *turned = call(
        forward_kernel,
        "forward_rows",
        [((512, 1024), F32), ((STEPS, 512, CHUNK), F32), ((512, 768), BF16)] + [((1024, 512), BF16)] * 4,
        (moved, near, noise_weight, gain, w_in, w_out),
        "mmamaa",
        "hhmmmmm",
        [
            pltpu.VMEM((512, 1024), F32),
            pltpu.VMEM((STEPS, 512, CHUNK), F32),
            pltpu.VMEM((2, 512, CHUNK), F32),
            pltpu.VMEM((512, 768), F32),
            pltpu.SemaphoreType.DMA((STEPS,)),
            pltpu.SemaphoreType.DMA,
            pltpu.VMEM((1024, 4096 - NEAR), BF16),
            pltpu.VMEM((4096, 768), BF16),
            pltpu.VMEM((128, 1024), BF16),
            pltpu.SemaphoreType.DMA,
            pltpu.SemaphoreType.DMA((2,)),
            pltpu.SemaphoreType.DMA,
        ],
        flops=2 * 512 * 4096 * (1024 + 768),
        limit=32,
    )
    theirs = [swap_core(piece) for piece in turned]
    high, low, own, other = call(
        score_kernel,
        "score_rows",
        [((512, 768), BF16)] * 4,
        (core, pred, observed),
        "smm",
        "hhmm",
        [pltpu.VMEM((32, 16, 768), F32)] * 2 + [pltpu.VMEM((512, 768), BF16)] * 2 + [pltpu.SemaphoreType.DMA((2,))],
        flops=2 * 512 * 4096 * 1024,
        limit=10,
    )
    got = swap_core(other)
    begun = make_outer("outer_own", 1, device, (own,), (turned,))
    send = make_outer("outer_send", 1, device, (got,), (theirs,), begun)
    came = [swap_stage(send[part], part, 0) for part in range(3)]
    keep = make_outer("outer_keep", 0, device, (own, got), (turned, theirs))
    begun = make_back(0, high, low, w_out, w_in, slope)
    *came, begun = lax.optimization_barrier((*came, begun))

    send = [keep[part][1024:] + came[part][1024:] for part in range(3)]
    after = [swap_stage(send[part], part, 1) for part in range(3)]
    keep = [keep[part][:1024] + came[part][:1024] for part in range(3)]
    latent = make_back(STEPS // 2, high, low, w_out, w_in, slope, begun, cond, gain)
    *came, latent = lax.optimization_barrier((*after, latent))

    send = [keep[part][512:] + came[part][512:] for part in range(3)]
    after = [swap_stage(send[part], part, 2) for part in range(3)]
    keep = [keep[part][:512] + came[part][:512] for part in range(3)]
    beside = swap_core(latent)
    (packed,) = call(
        pack_kernel, "pack", [((8, 224, 128), F32)], (*keep, *after, latent, beside), "mmmmmmmm", "m"
    )
    got = lax.all_to_all(
        packed, AXES, split_axis=0, concat_axis=0, tiled=True, axis_index_groups=last_groups()
    )
    mine, give, latent = call(
        sum_kernel, "sum_blocks", [((96, 128), F32), ((224, 128), F32), ((128, 128), F32)], (core, got), "sm", "mmm"
    )
    given = swap_core(give)
    return tuple(
        call(
            place_kernel,
            "place_blocks",
            [((32, 768), F32), ((128, 128), F32)],
            (core, mine, given, latent),
            "smmm",
            "mm",
        )
    )


def solution(mesh):
    placed = (
        P("token", "member"),
        P("member", "token", None),
        P(),
        P(),
        P(),
        P(),
        P(("token", "member"), None),
    )
    return jax.shard_map(
        per_device,
        mesh=mesh,
        in_specs=placed,
        out_specs=(P(("member", "token"), None), P("token", "member")),
        check_vma=False,
    )
```

```python
import functools

import jax
import jax.numpy as jnp
import numpy as np
from jax import lax
from jax.experimental import pallas as pl
from jax.experimental.pallas import tpu as pltpu
from jax.sharding import PartitionSpec as P

AXES = ("member", "token")
FIRST = (("x0", "x1", "z1"), ("y0", "y1", "z0"))
CHUNK = 512
NEAR = 1024
STEPS = 4096 // CHUNK
F32, BF16 = jnp.float32, jnp.bfloat16
LAST = (((1,), (1,)), ((), ()))


def coords(index):
    member, token = divmod(index, 16)
    y, z_lo = divmod(member, 2)
    z_hi, x, core = token // 8, token // 2 % 4, token % 2
    return {"x": x, "y": y, "z": 2 * z_hi + z_lo}, core


def index_of(place, core):
    return (place["y"] * 2 + place["z"] % 2) * 16 + (place["z"] // 2) * 8 + place["x"] * 2 + core


def order_of(core, part):
    return FIRST[core][part:] + FIRST[core][:part]


def group_place(index):
    place, core = coords(index)
    if core == 0:
        return (0, place["x"], place["z"] // 2), place["y"] * 2 + place["z"] % 2
    return (1, place["y"], place["z"] % 2 ^ place["z"] // 2), place["z"] // 2 * 4 + place["x"]


def last_groups():
    groups = {}
    for index in range(128):
        group, at = group_place(index)
        groups.setdefault(group, [None] * 8)[at] = index
    return [groups[name] for name in sorted(groups)]


def shift_of(core, part, group):
    bits = {dim: group >> (2 - at) & 1 for at, dim in enumerate(order_of(core, part))}
    if core == 0:
        return bits["z1"] * 4 + bits["x1"] * 2 + (bits["x0"] ^ bits["x1"])
    return (bits["y1"] * 2 + (bits["y0"] ^ bits["y1"])) * 16 + bits["z0"] * 8


def chip_at(device, part, place):
    group, at = divmod(place, 8)
    chip = device // 2
    low = at * 8 + ((chip & 7) ^ shift_of(0, part, group))
    lean = (chip >> 3 ^ chip >> 2) & 1
    line = ((chip & 48) + lean * 8) ^ (shift_of(1, part, group) ^ (at >> 2) * 8)
    return jnp.where(device % 2 == 0, low, line + at)


def partner(index, dim):
    place, core = coords(index)
    place[dim[0]] ^= 1 if dim[1] == "0" else 3
    return index_of(place, core)


def swap_stage(values, part, stage):
    pairs = [(i, partner(i, order_of(i % 2, part)[stage])) for i in range(128)]
    return lax.ppermute(values, AXES, pairs)


def swap_core(values):
    return lax.ppermute(values, AXES, [(i, i ^ 1) for i in range(128)])


def call(body, name, outs, args, spaces, out_spaces, scratch=(), flops=0, limit=16):
    placed = [
        pltpu.with_memory_space_constraint(a, {"v": pltpu.VMEM, "a": pltpu.HBM}[space]) if space in "va" else a
        for a, space in zip(args, spaces)
    ]
    kinds = {"s": pltpu.SMEM, "v": pltpu.VMEM, "m": pltpu.VMEM, "a": pltpu.HBM, "h": pltpu.HBM}
    return pl.pallas_call(
        body,
        in_specs=[pl.BlockSpec(memory_space=kinds[space]) for space in spaces],
        out_specs=[pl.BlockSpec(memory_space=kinds[space]) for space in out_spaces],
        out_shape=[
            {"v": pltpu.VMEM, "h": pltpu.HBM, "m": jax.ShapeDtypeStruct}[space](shape, kind)
            for (shape, kind), space in zip(outs, out_spaces)
        ],
        scratch_shapes=list(scratch),
        compiler_params=pltpu.CompilerParams(vmem_limit_bytes=limit * 1024 * 1024),
        cost_estimate=pl.CostEstimate(
            flops=flops, bytes_accessed=sum(a.size * a.dtype.itemsize for a in args), transcendentals=0
        ),
        name=name,
    )(*placed)


def gather_kernel(noise_hbm, latents_hbm, out_ref, noise_ref, latents_ref, sems):
    copies = [
        pltpu.make_async_copy(noise_hbm, noise_ref, sems.at[0]),
        pltpu.make_async_copy(latents_hbm, latents_ref, sems.at[1]),
    ]
    for copy in copies:
        copy.start()
    for copy in copies:
        copy.wait()
    for j in range(8):
        rows = slice(j * 16, j * 16 + 16)
        for i in range(4):
            out_ref[j, i] = noise_ref[i, rows, :]
        out_ref[j, 4] = latents_ref[rows, :]


def fetch_kernel(w_in_hbm, near_ref, sem):
    copy = pltpu.make_async_copy(w_in_hbm.at[:, 0:NEAR], near_ref, sem)
    copy.start()
    copy.wait()


def forward_kernel(moved_ref, near_ref, nw_hbm, gain_ref, w_in_hbm, w_out_hbm, cond_hbm, slope_hbm, pred_ref, *rest):
    turned = rest[:4]
    cond_ref, slope_ref, pre_ref, total_ref, out_sems, cond_sem = rest[4:10]
    w_in_ref, w_out_ref, nw_ref, in_sem, mid_sems, nw_sem = rest[10:]

    def columns(step):
        return slice(step * CHUNK, (step + 1) * CHUNK)

    def put(step):
        return pltpu.make_async_copy(slope_ref.at[step], slope_hbm.at[step], out_sems.at[step])

    fetch_in = pltpu.make_async_copy(w_in_hbm.at[:, NEAR:], w_in_ref, in_sem)
    fetch_out = [
        pltpu.make_async_copy(w_out_hbm.at[rows, :], w_out_ref.at[rows, :], mid_sems.at[i])
        for i, rows in enumerate((slice(0, NEAR), slice(NEAR, 4096)))
    ]
    fetch_nw = pltpu.make_async_copy(nw_hbm, nw_ref, nw_sem)
    fetch_nw.start()
    fetch_out[0].start()
    fetch_in.start()
    fetch_out[1].start()
    moved = moved_ref[...]
    noise = moved[:, :4].reshape(512, 128)
    latents = jnp.concatenate([moved[j, 4] for j in range(8)], axis=1).astype(F32)
    fetch_nw.wait()
    cond = jnp.dot(noise, nw_ref[...], preferred_element_type=F32)
    cond = (cond.reshape(32, 16, 1024) + latents[None]).reshape(512, 1024)
    scale = lax.rsqrt(jnp.mean(cond * cond, axis=-1, keepdims=True) + 1e-05)
    cond_ref[...] = cond
    put_cond = pltpu.make_async_copy(cond_ref, cond_hbm, cond_sem)
    put_cond.start()
    normed = (cond * scale * gain_ref[...].astype(F32)).astype(BF16)
    root = np.float32(np.sqrt(2 / np.pi))
    cubic = np.float32(np.sqrt(2 / np.pi) * 0.044715)
    for step in range(STEPS + 1):
        if step == NEAR // CHUNK:
            fetch_in.wait()
        if step < NEAR // CHUNK:
            pre_ref[step % 2] = jnp.dot(normed, near_ref[:, columns(step)], preferred_element_type=F32)
        elif step < STEPS:
            at = slice(step * CHUNK - NEAR, (step + 1) * CHUNK - NEAR)
            pre_ref[step % 2] = jnp.dot(normed, w_in_ref[:, at], preferred_element_type=F32)
        if step == 1:
            fetch_out[0].wait()
        if step == NEAR // CHUNK + 1:
            fetch_out[1].wait()
        if step > 0:
            done = step - 1
            pre = pre_ref[done % 2]
            square = pre * pre
            bend = jnp.tanh(pre * (root + cubic * square))
            cdf = 0.5 + 0.5 * bend
            value = pre * cdf
            hidden = value.astype(BF16)
            slope_ref[done] = cdf + (value - value * cdf) * (2.0 * root + 6.0 * cubic * square)
            flipped = hidden.T.reshape(8, 4, 16, 512)
            for i in range(4):
                turned[i][done * 128 : done * 128 + 128, :] = flipped[:, i].reshape(128, 512)
            put(done).start()
            term = jnp.dot(hidden, w_out_ref[columns(done), :], preferred_element_type=F32)
            if done == 0:
                total_ref[...] = term
            elif done < STEPS - 1:
                total_ref[...] += term
            else:
                pred_ref[...] = (total_ref[...] + term).astype(BF16)
    put_cond.wait()
    for step in range(STEPS):
        put(step).wait()


def score_kernel(core_ref, pred_in_ref, target_ref, high_hbm, low_hbm, own_ref, other_ref, pred_ref, grad_ref, high_ref, low_ref, sems):
    pred_ref[...] = pred_in_ref[...].astype(F32).reshape(32, 16, 768)
    grad_ref[...] = jnp.zeros_like(grad_ref)

    for member in range(32):
        own = pred_ref[member]
        total = jnp.zeros((16, 768), F32)
        for offset in range(1, 17 if member < 16 else 16):
            other = (member + offset) % 32
            diff = own - pred_ref[other]
            push = diff * lax.rsqrt(jnp.mean(diff * diff, axis=-1, keepdims=True) + 1e-06)
            grad_ref[other] -= push
            total = total + push
        grad_ref[member] += total
    err = pred_ref[...] - target_ref[...].astype(F32)[None]
    inverse = lax.rsqrt(jnp.mean(err * err, axis=-1, keepdims=True) + 1e-06)
    grad = (err * inverse - grad_ref[...] * (1.0 / 32)).reshape(512, 768)
    high = grad.astype(BF16)
    low = (grad - high.astype(F32)).astype(BF16)
    high_ref[...] = high
    low_ref[...] = low
    copies = [
        pltpu.make_async_copy(high_ref, high_hbm, sems.at[0]),
        pltpu.make_async_copy(low_ref, low_hbm, sems.at[1]),
    ]
    for copy in copies:
        copy.start()

    def halves(mine_ref, yours_ref):
        for part in range(3):
            at = part * 128
            mine_ref[:, 2 * at : 2 * at + 128] = high[:, at : at + 128]
            mine_ref[:, 2 * at + 128 : 2 * at + 256] = low[:, at : at + 128]
            yours_ref[:, 2 * at : 2 * at + 128] = high[:, 384 + at : 512 + at]
            yours_ref[:, 2 * at + 128 : 2 * at + 256] = low[:, 384 + at : 512 + at]

    @pl.when(core_ref[0] == 0)
    def _():
        halves(own_ref, other_ref)

    @pl.when(core_ref[0] == 1)
    def _():
        halves(other_ref, own_ref)

    for copy in copies:
        copy.wait()


def outer_kernel(side, sources, added, device_ref, *refs):
    grads, refs = refs[:sources], refs[sources:]
    turned, refs = [refs[4 * i : 4 * i + 4] for i in range(sources)], refs[4 * sources :]
    before, refs = refs[: 3 * added], refs[3 * added :]
    outs, rows_refs = refs[:3], refs[3:]
    for part in range(3):
        fields = slice(part * 256, part * 256 + 256)
        for quarter in range(4):
            at = slice(quarter * 512, quarter * 512 + 512)
            for block in range(8):
                chip = chip_at(device_ref[0], part, side * 32 + quarter * 8 + block)
                rows = pl.ds(pl.multiple_of(chip * 16, 16), 16)
                for i in range(4):
                    first = quarter * 512 + block * 64 + i * 16
                    for source in range(sources):
                        rows_refs[source][first : first + 16, :] = turned[source][i][rows, :]
            both = jnp.dot(rows_refs[0][at, :], grads[0][:, fields], preferred_element_type=F32)
            for source in range(1, sources):
                both += jnp.dot(rows_refs[source][at, :], grads[source][:, fields], preferred_element_type=F32)
            total = both[:, :128] + both[:, 128:]
            outs[part][at, :] = total + before[part][at, :] if added else total


def make_outer(name, side, device, grads, turned, before=()):
    n = len(grads)
    pieces = [piece for pieces in turned for piece in pieces]
    return call(
        functools.partial(outer_kernel, side, n, len(before) // 3),
        name,
        [((2048, 128), F32)] * 3,
        (device, *grads, *pieces, *before),
        "s" + "m" * (5 * n + len(before)),
        "mmm",
        [pltpu.VMEM((2048, 512), BF16)] * n,
        flops=2 * 512 * n * 256 * 2048 * 3,
        limit=8,
    )


def back_kernel(begin, high_ref, low_ref, w_out_ref, w_in_ref, slope_ref, *rest):
    if begin == 0:
        (total_ref,) = rest
    else:
        before_ref, cond_ref, gain_ref, out_ref, total_ref = rest
    for step in range(begin, begin + STEPS // 2):
        columns = slice(step * CHUNK, (step + 1) * CHUNK)
        w_out = w_out_ref[columns, :]
        back = lax.dot_general(high_ref[...], w_out, LAST, preferred_element_type=F32)
        back += lax.dot_general(low_ref[...], w_out, LAST, preferred_element_type=F32)
        dpre = (back * slope_ref[step]).astype(BF16)
        term = lax.dot_general(dpre, w_in_ref[:, columns], LAST, preferred_element_type=F32)
        if step == 0:
            total_ref[...] = term
        elif step == begin:
            total_ref[...] = before_ref[...] + term
        else:
            total_ref[...] += term
    if begin == 0:
        return
    cond = cond_ref[...]
    scale = lax.rsqrt(jnp.mean(cond * cond, axis=-1, keepdims=True) + 1e-05)
    weighted = total_ref[...] * gain_ref[...].astype(F32)
    mean = jnp.mean(weighted * cond, axis=-1, keepdims=True)
    dcond = scale * weighted - cond * (scale * scale * scale * mean)
    total = jnp.sum(dcond.reshape(32, 16, 1024), axis=0)
    for j in range(8):
        out_ref[j] = total[:, j * 128 : j * 128 + 128]


def make_back(begin, high, low, w_out, w_in, slope, *more):
    (out,) = call(
        functools.partial(back_kernel, begin),
        "back_end" if begin else "back_begin",
        [((8, 16, 128) if begin else (512, 1024), F32)],
        (high, low, w_out, w_in, slope) + more,
        "m" * (5 + len(more)),
        "m",
        [pltpu.VMEM((512, 1024), F32)] if begin else [],
        flops=512 * 4096 * (768 * 2 + 1024),
        limit=10,
    )
    return out


def pack_kernel(*refs):
    keep, came, (mine_ref, theirs_ref, out_ref) = refs[:3], refs[3:6], refs[6:]
    for part in range(3):
        for j in range(8):
            rows = slice(j * 64, j * 64 + 64)
            out_ref[j, part * 64 : part * 64 + 64, :] = keep[part][rows, :] + came[part][rows, :]
    out_ref[:, 192:208, :] = mine_ref[...]
    out_ref[:, 208:224, :] = theirs_ref[...]


def sum_kernel(core_ref, got_ref, mine_ref, give_ref, latent_ref):
    total = got_ref[0, :192, :]
    for j in range(1, 8):
        total += got_ref[j, :192, :]
    latent_ref[...] = got_ref[:, 192:208, :].reshape(128, 128)
    give_ref[96:, :] = got_ref[:, 208:224, :].reshape(128, 128)
    low = core_ref[0] == 0
    for part in range(3):
        top = total[part * 64 : part * 64 + 32]
        bottom = total[part * 64 + 32 : part * 64 + 64]
        mine_ref[part * 32 : part * 32 + 32, :] = jnp.where(low, top, bottom)
        give_ref[part * 32 : part * 32 + 32, :] = jnp.where(low, bottom, top)


def place_kernel(core_ref, mine_ref, given_ref, latent_ref, grad_ref, out_ref):
    low = core_ref[0] == 0
    for part in range(3):
        mine = mine_ref[part * 32 : part * 32 + 32, :]
        given = given_ref[part * 32 : part * 32 + 32, :]
        grad_ref[:, part * 128 : part * 128 + 128] = jnp.where(low, mine, given)
        grad_ref[:, 384 + part * 128 : 512 + part * 128] = jnp.where(low, given, mine)
    out_ref[...] = jnp.where(low, latent_ref[...], given_ref[96:, :])


def per_device(latents, noise, noise_weight, gain, w_in, w_out, observed):
    device = lax.axis_index(AXES)
    core = (device % 2).reshape(1)
    device = device.reshape(1)
    gain = gain.reshape(1, 1024)

    noise, latents, device, core = lax.optimization_barrier((noise, latents, device, core))
    (moved,) = call(gather_kernel, "gather_in", [((8, 5, 16, 128), BF16)], (noise, latents), "aa", "m", [pltpu.VMEM((4, 128, 128), BF16), pltpu.VMEM((128, 128), BF16), pltpu.SemaphoreType.DMA((2,))])
    moved = lax.all_to_all(moved, "member", split_axis=0, concat_axis=0, tiled=True)
    (near,) = call(
        fetch_kernel, "fetch_near", [((1024, NEAR), BF16)], (w_in,), "a", "m", [pltpu.SemaphoreType.DMA], limit=1
    )
    cond, slope, pred, *turned = call(
        forward_kernel,
        "forward_rows",
        [((512, 1024), F32), ((STEPS, 512, CHUNK), F32), ((512, 768), BF16)] + [((1024, 512), BF16)] * 4,
        (moved, near, noise_weight, gain, w_in, w_out),
        "mmamaa",
        "hhmmmmm",
        [
            pltpu.VMEM((512, 1024), F32),
            pltpu.VMEM((STEPS, 512, CHUNK), F32),
            pltpu.VMEM((2, 512, CHUNK), F32),
            pltpu.VMEM((512, 768), F32),
            pltpu.SemaphoreType.DMA((STEPS,)),
            pltpu.SemaphoreType.DMA,
            pltpu.VMEM((1024, 4096 - NEAR), BF16),
            pltpu.VMEM((4096, 768), BF16),
            pltpu.VMEM((128, 1024), BF16),
            pltpu.SemaphoreType.DMA,
            pltpu.SemaphoreType.DMA((2,)),
            pltpu.SemaphoreType.DMA,
        ],
        flops=2 * 512 * 4096 * (1024 + 768),
        limit=32,
    )
    theirs = [swap_core(piece) for piece in turned]
    high, low, own, other = call(
        score_kernel,
        "score_rows",
        [((512, 768), BF16)] * 4,
        (core, pred, observed),
        "smm",
        "hhmm",
        [pltpu.VMEM((32, 16, 768), F32)] * 2 + [pltpu.VMEM((512, 768), BF16)] * 2 + [pltpu.SemaphoreType.DMA((2,))],
        flops=2 * 512 * 4096 * 1024,
        limit=10,
    )
    got = swap_core(other)
    begun = make_outer("outer_own", 1, device, (own,), (turned,))
    send = make_outer("outer_send", 1, device, (got,), (theirs,), begun)
    came = [swap_stage(send[part], part, 0) for part in range(3)]
    keep = make_outer("outer_keep", 0, device, (own, got), (turned, theirs))
    begun = make_back(0, high, low, w_out, w_in, slope)
    came[2], begun = lax.optimization_barrier((came[2], begun))

    send = [keep[part][1024:] + came[part][1024:] for part in range(3)]
    after = [swap_stage(send[part], part, 1) for part in range(3)]
    keep = [keep[part][:1024] + came[part][:1024] for part in range(3)]
    latent = make_back(STEPS // 2, high, low, w_out, w_in, slope, begun, cond, gain)
    came = after
    came[2], latent = lax.optimization_barrier((came[2], latent))

    send = [keep[part][512:] + came[part][512:] for part in range(3)]
    after = [swap_stage(send[part], part, 2) for part in range(3)]
    keep = [keep[part][:512] + came[part][:512] for part in range(3)]
    beside = swap_core(latent)
    (packed,) = call(
        pack_kernel, "pack", [((8, 224, 128), F32)], (*keep, *after, latent, beside), "mmmmmmmm", "m"
    )
    got = lax.all_to_all(
        packed, AXES, split_axis=0, concat_axis=0, tiled=True, axis_index_groups=last_groups()
    )
    mine, give, latent = call(
        sum_kernel, "sum_blocks", [((96, 128), F32), ((224, 128), F32), ((128, 128), F32)], (core, got), "sm", "mmm"
    )
    given = swap_core(give)
    return tuple(
        call(
            place_kernel,
            "place_blocks",
            [((32, 768), F32), ((128, 128), F32)],
            (core, mine, given, latent),
            "smmm",
            "mm",
        )
    )


def solution(mesh):
    placed = (
        P("token", "member"),
        P("member", "token", None),
        P(),
        P(),
        P(),
        P(),
        P(("token", "member"), None),
    )
    return jax.shard_map(
        per_device,
        mesh=mesh,
        in_specs=placed,
        out_specs=(P(("member", "token"), None), P("token", "member")),
        check_vma=False,
    )
```
